32 devices in a mesh: owner: 4 (over y, x), worker: 8 (over z, core).
Axes of the slice: x: 2, y: 2, z: 4, core: 2. Of those that a mesh axis runs over, the one named last changes fastest.
Arguments:
- states: float32 [65536, 512], P(('owner', 'worker')), may hold values from -3 to 3
- row_of_user: int32 [65536], replicated, may hold values from 0 to 65535, as said below
- event_users: int32 [16384], P(('owner', 'worker')), may hold values from 0 to 65535, as said below
- event_features: int32 [16384], P(('owner', 'worker')), may hold values from 0 to 4095
- feature_table: bfloat16 [4096, 512], replicated, may hold values from -6 to 6
- gate_in: bfloat16 [512, 1536], replicated, may hold values from -0.25 to 0.25
- gate_state: bfloat16 [512, 1536], replicated, may hold values from -0.25 to 0.25
- tower_in: bfloat16 [4096, 1024], P(('owner', 'worker')), may hold values from -0.1875 to 0.1875
- tower_out: bfloat16 [512, 4096], P(('owner', 'worker')), may hold values from -0.09375 to 0.09375
Outputs:
- new_states: float32 [65536, 512], P(('owner', 'worker'))
- scores: float32 [16384], P(('owner', 'worker'))
The draws below stay inside these ranges and needn't reach their ends.
Inputs may be any that keep to these rules, and one draw needn't show every extreme that they name: `row_of_user`: A permutation: each user has its own state row. `event_users`: among the 512 events of one device, at most 32 have their row (row_of_user of the user) in one device's block of 2048 rows, and for every device some block receives exactly 32 of its events.
All inputs are finite; a program needn't handle non-finite values.
Results may differ from the reference program's by a relative error of at most 0.0034.
Values may be sent and summed in bfloat16 or wider, within the bound.
No kernel may reach another device: no remote copies, remote signals or barrier semaphores. Data moves between devices by JAX's collectives and lax.ppermute only.
A program may use at most 128 MiB of HBM per device.

```python
import math
import jax
import jax.numpy as jnp
import numpy as np
from jax import lax

S = 512
HID = 4096
FEATS = 4096
U_DEV = 2048
EV_DEV = 512
SHARDS = 32
USERS = 65536
EVENTS = 16384
MEAN_SLOTS = 16


def joint_draw(key):
    row_of_user = jax.random.permutation(jax.random.fold_in(key, 11), USERS).astype(jnp.int32)
    hot = jax.random.randint(jax.random.fold_in(key, 12), (SHARDS,), 0, 2)
    noise = jax.random.randint(jax.random.fold_in(key, 13), (SHARDS, SHARDS), 0, 1024)
    score = (noise + hot[None, :] * 1024) * SHARDS + jnp.arange(SHARDS)[None, :]
    ranked = jnp.argsort(-score, axis=1).astype(jnp.int32)
    slot = jnp.arange(EV_DEV)
    half = EV_DEV // 2
    place = jnp.where(slot < half, slot // (2 * MEAN_SLOTS), SHARDS // 4 + (slot - half) // MEAN_SLOTS)
    target = ranked[:, place]
    mixer = jax.random.randint(jax.random.fold_in(key, 14), (SHARDS, EV_DEV), 0, 4096) * EV_DEV + slot[None, :]
    order = jnp.argsort(mixer, axis=1)
    target = jnp.take_along_axis(target, order, axis=1)
    local = jax.random.randint(jax.random.fold_in(key, 15), (SHARDS, EV_DEV), 0, U_DEV)
    rows = (target * U_DEV + local).reshape(EVENTS)
    user_of_row = jnp.zeros((USERS,), jnp.int32).at[row_of_user].set(jnp.arange(USERS, dtype=jnp.int32))
    return (row_of_user, user_of_row[rows].astype(jnp.int32))


def draw_row_of_user(key, part):
    return joint_draw(key)[0]


def draw_event_users(key, part):
    return joint_draw(key)[1]


def with_ends(drawn, rng, low, high):
    dims = drawn.shape
    index_at = [jax.random.randint(jax.random.fold_in(rng, axis), (), 0, dims[axis]) for axis in range(len(dims))]
    drawn = drawn.at[tuple(index_at)].set(low)
    longest = dims.index(max(dims))
    index_at[longest] = (index_at[longest] + 1) % dims[longest]
    return drawn.at[tuple(index_at)].set(high)


def level_of(key, dims, cuts, least, high):
    def one(axis_at, blocks):
        heights = jax.random.uniform(jax.random.fold_in(jax.random.fold_in(key, 6), axis_at), (blocks,), jnp.float32, least / len(cuts), high / len(cuts))
        return jnp.repeat(jnp.exp(heights), dims[axis_at] // blocks).reshape((-1,) + (1,) * (len(dims) - axis_at - 1))

    gain = one(*cuts[0])
    for cut in cuts[1:]:
        gain = gain * one(*cut)
    return gain


def cumulative_ranks(number_of, lean):
    loads = [(1 << 20) // math.isqrt(standing ** lean) + 1 for standing in range(1, number_of + 1)]
    scale = 1 + sum(loads) // (1 << 30)
    return np.cumsum(np.array([max(1, weight // scale) for weight in loads]))


def ranked_ids(rng, shape, number_of, lean):
    listing = cumulative_ranks(number_of, lean)
    ticket = jax.random.randint(jax.random.fold_in(rng, 1), shape, 0, int(listing[number_of - 1]))
    grade = jnp.searchsorted(jnp.asarray(listing, jnp.int32), ticket, side="right")
    return jax.random.permutation(jax.random.fold_in(rng, 2), number_of)[grade].astype(jnp.int32)


def normal_values(key, extent, deviation, bound, pieces=(), held_as=jnp.bfloat16):
    drawn = jax.random.normal(key, extent, jnp.float32) * deviation
    if len(pieces) > 0:
        drawn = level_of(key, extent, pieces, -0.22, 0.18) * drawn
    return jnp.clip(drawn, min=-bound, max=bound).astype(held_as)


def setup_inputs(seed: int = 0) -> dict:
    arg_keys = jax.random.split(jax.random.key(seed), 10)
    return {
        "states": normal_values(arg_keys[0], (USERS, S), 0.5, 3.0, ((0, 32),), jnp.float32),
        "row_of_user": draw_row_of_user(jax.random.fold_in(arg_keys[9], 71), 0),
        "event_users": draw_event_users(jax.random.fold_in(arg_keys[9], 71), 0),
        "event_features": with_ends(ranked_ids(arg_keys[3], (EVENTS,), FEATS, 2), jax.random.fold_in(arg_keys[3], 3), 0, FEATS - 1).astype(jnp.int32),
        "feature_table": normal_values(arg_keys[4], (FEATS, S), 1.0, 6.0),
        "gate_in": normal_values(arg_keys[5], (S, 3 * S), S ** -0.5, 0.25),
        "gate_state": normal_values(arg_keys[6], (S, 3 * S), S ** -0.5, 0.25),
        "tower_in": normal_values(arg_keys[7], (HID, 2 * S), (2 * S) ** -0.5, 0.1875, ((0, 32),)),
        "tower_out": normal_values(arg_keys[8], (S, HID), HID ** -0.5, 0.09375, ((0, 32),)),
    }


def gru_cell(inputs, prior, gate_in, gate_state):
    gx = jnp.dot(inputs, gate_in, preferred_element_type=jnp.float32)
    gh = jnp.dot(prior, gate_state, preferred_element_type=jnp.float32)
    width = prior.shape[-1]
    reset = jax.nn.sigmoid(gx[:, :width] + gh[:, :width])
    update = jax.nn.sigmoid(gx[:, width:2 * width] + gh[:, width:2 * width])
    cand = jnp.tanh(gx[:, 2 * width:] + reset * gh[:, 2 * width:])
    return (1.0 - update) * cand + update * prior.astype(jnp.float32)

def reference(states, row_of_user, event_users, event_features, feature_table, gate_in, gate_state, tower_in, tower_out):
    rows = row_of_user[event_users]
    prior = states[rows].astype(jnp.bfloat16)
    inputs = feature_table[event_features]

    def block(pair):
        x_blk, h_blk = pair
        fresh = gru_cell(x_blk, h_blk, gate_in, gate_state)
        joined = jnp.concatenate([fresh.astype(jnp.bfloat16), x_blk], axis=1)
        hidden = jax.nn.gelu(lax.dot_general(joined, tower_in, (((1,), (1,)), ((), ())), preferred_element_type=jnp.float32)).astype(jnp.bfloat16)
        tower = lax.dot_general(hidden, tower_out, (((1,), (1,)), ((), ())), preferred_element_type=jnp.float32)
        score = lax.optimization_barrier(jnp.sum(tower * x_blk.astype(jnp.float32), axis=1)) / jnp.sqrt(jnp.float32(S))
        return (score, fresh - h_blk.astype(jnp.float32))
    scores, delta = lax.map(block, (inputs.reshape(SHARDS, EV_DEV, S), prior.reshape(SHARDS, EV_DEV, S)))
    total = jax.ops.segment_sum(delta.reshape(EVENTS, S), rows, num_segments=USERS)
    count = jax.ops.segment_sum(jnp.ones((EVENTS,), jnp.int32), rows, num_segments=USERS)
    new_states = states + total / jnp.maximum(count, 1).astype(jnp.float32)[:, None]
    return (new_states, scores.reshape(EVENTS))
```

```python
import functools

import jax
import jax.numpy as jnp
from jax import lax
from jax.experimental import pallas as pl
from jax.experimental.pallas import tpu as pltpu
from jax.sharding import PartitionSpec as P

AXES = ("owner", "worker")
LANES = 128
CHUNK = 256
F32 = jnp.float32
BF16 = jnp.bfloat16
I32 = jnp.int32
VMEM = pl.BlockSpec(memory_space=pltpu.VMEM)
ANY = pl.BlockSpec(memory_space=pl.ANY)
HBM = pl.BlockSpec(memory_space=pltpu.HBM)


def iota(shape, axis):
    return lax.broadcasted_iota(I32, shape, axis)


def onehot(mask):
    return jnp.where(mask, 1.0, 0.0).astype(BF16)


def dot(a, b, ca=1, cb=0):
    return lax.dot_general(a, b, (((ca,), (cb,)), ((), ())), preferred_element_type=F32)


def split3(x):
    a = x.astype(BF16)
    r = x - a.astype(F32)
    b = r.astype(BF16)
    return a, b, (r - b.astype(F32)).astype(BF16)


def route_kernel(table_hbm, users_ref, feats_ref, *refs, shards, cap, row_count, chips):
    table_ref, sem = refs[-2:]
    copy = pltpu.make_async_copy(table_hbm, table_ref, sem)
    copy.start()
    if chips:
        wout_ref, req_ref, slot_ref, mine_ref, theirs_ref = refs[:5]
        owners, depth = chips
        units = wout_ref.shape[1] // (2 * owners * depth)
        rows = wout_ref.shape[0]
        even = lax.axis_index("worker") % 2 == 0
        for place in range(depth):
            for owner in range(owners):
                at = 2 * units * (owner * depth + place)
                a, b = wout_ref[:, at : at + units], wout_ref[:, at + units : at + 2 * units]
                to = units * ((place % (depth // 2)) * owners + owner)
                line = slice((place // (depth // 2)) * rows, (place // (depth // 2) + 1) * rows)
                mine_ref[line, to : to + units] = jnp.where(even, a, b)
                theirs_ref[line, to : to + units] = jnp.where(even, b, a)
    else:
        req_ref, slot_ref = refs[:2]
    users = users_ref[...]
    events = users.shape[1]
    high, low = users >> 7, users & 127
    pick = onehot(iota((table_ref.shape[0], events), 0) == high)
    copy.wait()
    table = table_ref[...]
    parts = [((table >> (8 * k)) & 255).astype(F32).astype(BF16) for k in range(3)]
    got = dot(jnp.concatenate(parts, axis=1), pick, 0, 0)
    here = iota((LANES, events), 0) == low
    row = jnp.zeros((1, events), F32)
    for k in range(3):
        part = jnp.where(here, got[k * LANES : (k + 1) * LANES], 0.0)
        row = row + float(256**k) * jnp.sum(part, axis=0, keepdims=True)
    row = row.astype(I32)
    device = iota((shards, events), 0)
    first = device * row_count
    mine = (row >= first) & (row < first + row_count)
    hit = jnp.where(mine, 1.0, 0.0)
    target = jnp.sum(jnp.where(mine, device, 0), axis=0, keepdims=True)
    local = row - target * row_count + 1
    before = onehot(iota((events, events), 0) < iota((events, events), 1))
    rank = dot(hit.astype(BF16), before)
    rank = jnp.sum(hit * rank, axis=0, keepdims=True).astype(I32)
    place = onehot(iota((cap, events), 0) == rank)
    feats = feats_ref[...]
    bytes_of = [(v & 255).astype(F32) for v in (local >> 8, local, feats >> 8, feats)]
    filled = dot(jnp.concatenate([hit * v for v in bytes_of], axis=0).astype(BF16), place, 1, 1)
    q = [filled[k * shards : (k + 1) * shards].astype(I32) for k in range(4)]
    req_ref[:, :cap] = q[0] * 256 + q[1]
    req_ref[:, cap:] = q[2] * 256 + q[3]
    slot_ref[:1, :] = target
    slot_ref[1:, :] = rank


def route(row_of_user, event_users, event_features, tower_out, shards, cap, row_count, chips):
    events = event_users.shape[0]
    table = row_of_user.reshape(-1, LANES)
    rows, hidden = tower_out.shape
    cut = [jax.ShapeDtypeStruct((2 * rows, hidden // 4), BF16)] * 2 if chips else []
    return pl.pallas_call(
        functools.partial(route_kernel, shards=shards, cap=cap, row_count=row_count, chips=chips),
        out_shape=[
            jax.ShapeDtypeStruct((shards, 2 * cap), I32),
            jax.ShapeDtypeStruct((2, events), I32),
            *cut,
        ],
        in_specs=[HBM, VMEM, VMEM] + [VMEM] * bool(chips),
        out_specs=[VMEM] * (2 + len(cut)),
        scratch_shapes=[pltpu.VMEM(table.shape, I32), pltpu.SemaphoreType.DMA],
        compiler_params=pltpu.CompilerParams(vmem_limit_bytes=24 * 2**20),
        cost_estimate=pl.CostEstimate(flops=10**9, bytes_accessed=10**6, transcendentals=0),
        name="route",
    )(table, event_users.reshape(1, events), event_features.reshape(1, events), *([tower_out] if chips else []))


def slot_column(asked, n, cap):
    shards = asked.shape[0]
    source = onehot(iota((n, shards), 0) // cap == iota((n, shards), 1))
    place = (iota((n, cap), 0) & (cap - 1)) == iota((n, cap), 1)
    wide = [dot(source, b.astype(F32).astype(BF16)) for b in (asked >> 8, asked & 255)]
    return jnp.sum(jnp.where(place, wide[0] * 256.0 + wide[1], 0.0), axis=1, keepdims=True).astype(I32)


def slot_row(asked, n, cap):
    shards = asked.shape[0]
    place = onehot((iota((cap, n), 1) & (cap - 1)) == iota((cap, n), 0))
    source = iota((shards, n), 1) // cap == iota((shards, n), 0)
    v = asked[:, :cap]
    wide = [dot(b.astype(F32).astype(BF16), place) for b in (v >> 8, v & 255)]
    return jnp.sum(jnp.where(source, wide[0] * 256.0 + wide[1], 0.0), axis=0, keepdims=True).astype(I32) - 1


def sigmoid(x):
    return 0.5 * jnp.tanh(0.5 * x) + 0.5


def fetch_kernel(asked_ref, table_hbm, *refs, cap, column):
    out_ref, table_ref, *low, sem = refs[-3 - (table_hbm.dtype != BF16) :]
    copy = pltpu.make_async_copy(table_hbm, table_ref, sem)
    copy.start()
    n, rows = out_ref.shape[0], table_hbm.shape[0]
    at_row = slot_column(asked_ref[:, column * cap : (column + 1) * cap], n, cap) - (1 - column)
    copy.wait()
    if low:
        low[0][...] = table_ref[...].astype(BF16)
    known = low[0] if low else table_ref
    for k in range(n // CHUNK):
        at = slice(k * CHUNK, (k + 1) * CHUNK)
        out_ref[at, :] = dot(onehot(iota((CHUNK, rows), 1) == at_row[at]), known[...]).astype(BF16)


def fetch(asked, table, cap, column, after=()):
    n, width = asked.shape[0] * cap, table.shape[1]
    low = [] if table.dtype == BF16 else [pltpu.VMEM(table.shape, BF16)]
    return pl.pallas_call(
        functools.partial(fetch_kernel, cap=cap, column=column),
        out_shape=jax.ShapeDtypeStruct((n, width), BF16),
        in_specs=[VMEM, HBM] + [ANY] * len(after),
        out_specs=VMEM,
        scratch_shapes=[pltpu.VMEM(table.shape, table.dtype), *low, pltpu.SemaphoreType.DMA],
        compiler_params=pltpu.CompilerParams(vmem_limit_bytes=32 * 2**20),
        cost_estimate=pl.CostEstimate(flops=2 * n * width * table.shape[0], bytes_accessed=5 * 10**6, transcendentals=0),
        name="fetch",
    )(asked, table, *after)


def cell_kernel(prior_ref, inputs_ref, gin_hbm, gst_hbm, *refs):
    fresh_ref, gin_ref, gst_ref, sems = refs[-4:]
    copies = [pltpu.make_async_copy(gst_hbm, gst_ref, sems.at[0]), pltpu.make_async_copy(gin_hbm, gin_ref, sems.at[1])]
    for copy in copies:
        copy.start()
    for copy in copies:
        copy.wait()
    n, width = fresh_ref.shape
    for k in range(n // CHUNK):
        at = slice(k * CHUNK, (k + 1) * CHUNK)
        prior = prior_ref[at, :]
        gh = dot(prior, gst_ref[...])
        gx = dot(inputs_ref[at, :], gin_ref[...])
        reset = sigmoid(gx[:, :width] + gh[:, :width])
        update = sigmoid(gx[:, width : 2 * width] + gh[:, width : 2 * width])
        cand = jnp.tanh(gx[:, 2 * width :] + reset * gh[:, 2 * width :])
        fresh = (1.0 - update) * cand + update * prior.astype(F32)
        fresh_ref[at, :] = fresh.astype(BF16)


def cell(prior, inputs, gate_in, gate_state, after=()):
    n, width = prior.shape
    return pl.pallas_call(
        cell_kernel,
        out_shape=jax.ShapeDtypeStruct((n, width), BF16),
        in_specs=[VMEM, VMEM, HBM, HBM] + [ANY] * len(after),
        out_specs=VMEM,
        scratch_shapes=[pltpu.VMEM(gate_in.shape, BF16)] * 2 + [pltpu.SemaphoreType.DMA((2,))],
        compiler_params=pltpu.CompilerParams(vmem_limit_bytes=32 * 2**20),
        cost_estimate=pl.CostEstimate(flops=4 * 10**9, bytes_accessed=6 * 10**6, transcendentals=2 * 10**6),
        name="cell",
    )(prior, inputs, gate_in, gate_state, *after)


def update_kernel(asked_ref, fresh_ref, states_ref, *refs, cap):
    out_ref, old_ref, new_ref, in_sems, out_sems = refs[-5:]
    n, rows = fresh_ref.shape[0], states_ref.shape[0]
    chunks = rows // CHUNK
    parts = [pl.ds(k * CHUNK, CHUNK) for k in range(chunks)]
    reads = [pltpu.make_async_copy(states_ref.at[p], old_ref.at[p], in_sems.at[k]) for k, p in enumerate(parts)]
    writes = [pltpu.make_async_copy(new_ref.at[p], out_ref.at[p], out_sems.at[k]) for k, p in enumerate(parts)]
    for read in reads:
        read.start()
    local = slot_row(asked_ref[...], n, cap)
    fresh = fresh_ref[...]
    ones = jnp.ones((n, LANES), BF16)
    for k in range(chunks):
        at = slice(k * CHUNK, (k + 1) * CHUNK)
        pick = onehot(iota((CHUNK, n), 0) + k * CHUNK == local)
        total = dot(pick, fresh)
        count = dot(pick, ones)[:, :1]
        reads[k].wait()
        old = old_ref[at, :]
        change = total / jnp.maximum(count, 1.0) - old.astype(BF16).astype(F32)
        new_ref[at, :] = old + jnp.where(count > 0.0, change, 0.0)
        writes[k].start()
    for write in writes:
        write.wait()


def update(asked, fresh, states, cap, after=()):
    chunks = states.shape[0] // CHUNK
    return pl.pallas_call(
        functools.partial(update_kernel, cap=cap),
        out_shape=jax.ShapeDtypeStruct(states.shape, F32),
        in_specs=[VMEM, VMEM, HBM] + [ANY] * len(after),
        out_specs=HBM,
        scratch_shapes=[pltpu.VMEM(states.shape, F32)] * 2 + [pltpu.SemaphoreType.DMA((chunks,))] * 2,
        compiler_params=pltpu.CompilerParams(vmem_limit_bytes=32 * 2**20),
        cost_estimate=pl.CostEstimate(flops=4 * 10**9, bytes_accessed=10**7, transcendentals=0),
        name="update",
    )(asked, fresh, states, *after)


def gelu(x):
    inner = 0.7978845608028654 * (x + 0.044715 * (x * x * x))
    return x * (0.5 * (1.0 + jnp.tanh(inner)))


def owner_at(flip):
    return lax.axis_index("owner") ^ flip


def depth_at(back, depth):
    return lax.rem(lax.axis_index("worker") // 2 + depth - back, depth)


def step_kernel(*refs, n_in, n_out, n_after, ins, outs, backs, rows, depth, cap, first, last):
    it = iter(refs)
    take = lambda k: [next(it) for _ in range(k)]
    fresh, inputs = take(2), take(2)
    before = None if first else next(it)
    in_refs, out_refs = take(n_in), take(n_out)
    take(n_after)
    line_ref, win_ref, wout_ref = take(3)
    groups, width, both = win_ref.shape
    half = both // 2
    chunk = fresh[0].shape[0]

    @pl.when(pl.program_id(0) == 0)
    def _():
        for group, index, count, flip, place in ins:
            owner = 0 if flip is None else owner_at(flip)
            at = pl.multiple_of(owner * rows[0] + place, 16)
            win_ref[group, pl.ds(at, count), :] = in_refs[index][...]
        if depth == 1:
            wout_ref[0] = out_refs[0][...]
        else:
            for index, start, flip, back in outs:
                chip = owner_at(flip) * depth + depth_at(back, depth)
                to = pl.ds(pl.multiple_of(chip * rows[1], 16), rows[1])
                for g, group_back in enumerate(backs):
                    place = depth_at(group_back, depth)
                    lanes = pl.ds(pl.multiple_of(lax.rem(place, 2) * width, LANES), width)
                    line = pl.ds(pl.multiple_of(start + rows[1] * (place // 2), 16), rows[1])
                    wout_ref[g, to, :] = out_refs[index][line, lanes]

    near = chunk // cap
    at = pl.ds(pl.multiple_of(pl.program_id(0) * near, near), near)
    for side in range(2):
        x, f = inputs[side][...], fresh[side][...]
        joined = jnp.concatenate([f, x], axis=1)
        tower = jnp.zeros((chunk, half), F32)
        for g in range(groups):
            h = gelu(dot(joined, win_ref[g], 1, 1)).astype(BF16)
            tower = tower + dot(h, wout_ref[g], 1, 1)
        score = jnp.sum(tower * x.astype(F32), axis=1, keepdims=True)
        place = (iota((chunk, cap), 0) & (cap - 1)) == iota((chunk, cap), 1)
        source = onehot(iota((near, chunk), 1) // cap == iota((near, chunk), 0))
        lines = sum(dot(source, p) for p in split3(jnp.where(place, score, 0.0)))
        lanes = slice(side * cap, (side + 1) * cap)
        if not first:
            lines = lines + before[at, lanes]
        if last:
            lines = lines / jnp.sqrt(F32(half))
        line_ref[at, lanes] = lines


def step(fresh, inputs, before, ins, outs, backs, rows, depth, cap, last, after=()):
    n, half = fresh[0].shape
    shards = n // cap
    chunk = min(n, 2 * CHUNK)
    in_parts = [(group, i, count, flip, place) for i, (group, _, count, flip, place) in enumerate(ins)]
    out_parts = [(i, start, flip, back) for i, (_, parts) in enumerate(outs) for start, flip, back in parts]
    width = sum(count for group, _, count, _, _ in ins if group == 0)
    side = pl.BlockSpec((chunk, half), lambda i: (i, 0))
    line = pl.BlockSpec((shards, 2 * cap), lambda i: (0, 0))
    whole = lambda a: pl.BlockSpec(a.shape, lambda i: (0, 0))
    units = len(backs) * width
    in_arrays, out_arrays = [a for _, a, _, _, _ in ins], [a for a, _ in outs]
    return pl.pallas_call(
        functools.partial(
            step_kernel,
            n_in=len(in_arrays),
            n_out=len(out_arrays),
            n_after=len(after),
            ins=in_parts,
            outs=out_parts,
            backs=backs,
            rows=rows,
            depth=depth,
            cap=cap,
            first=before is None,
            last=last,
        ),
        grid=(n // chunk,),
        out_shape=jax.ShapeDtypeStruct((shards, 2 * cap), F32),
        in_specs=[side] * 4
        + ([] if before is None else [line])
        + [whole(a) for a in in_arrays + out_arrays]
        + [ANY] * len(after),
        out_specs=line,
        scratch_shapes=[pltpu.VMEM((len(backs), width, 2 * half), BF16), pltpu.VMEM((len(backs), half, width), BF16)],
        compiler_params=pltpu.CompilerParams(vmem_limit_bytes=44 * 2**20),
        cost_estimate=pl.CostEstimate(flops=12 * n * units * half, bytes_accessed=10**7, transcendentals=2 * n * units),
        name="tower",
    )(*fresh, *inputs, *([] if before is None else [before]), *in_arrays, *out_arrays, *after)


def pick_kernel(back_ref, slot_ref, out_ref, *, cap):
    back = back_ref[...]
    shards = back.shape[0]
    target, rank = slot_ref[:1, :], slot_ref[1:, :]
    events = target.shape[1]
    place = onehot(iota((cap, events), 0) == rank)
    device = iota((shards, events), 0)
    score = jnp.zeros((shards, events), F32)
    for side in range(2):
        parts = split3(back[:, side * cap : (side + 1) * cap])
        here = device == (target if side == 0 else target + 1 - 2 * (target & 1))
        score = score + jnp.where(here, sum(dot(p, place) for p in parts), 0.0)
    out_ref[...] = jnp.sum(score, axis=0, keepdims=True)


def pick(back, slots, cap):
    return pl.pallas_call(
        functools.partial(pick_kernel, cap=cap),
        out_shape=jax.ShapeDtypeStruct((1, slots.shape[1]), F32),
        in_specs=[VMEM] * 2,
        out_specs=VMEM,
        cost_estimate=pl.CostEstimate(flops=10**8, bytes_accessed=10**5, transcendentals=0),
        name="pick",
    )(back, slots)


def exchange(x):
    return lax.all_to_all(x, AXES, split_axis=0, concat_axis=0, tiled=True)


def send(x, devices, to):
    return lax.ppermute(x, AXES, [(d, to(d)) for d in range(devices)])


def by_core(mine, theirs, devices, axis):
    even = lax.axis_index("worker") % 2 == 0
    got = send(theirs, devices, lambda d: d ^ 1)
    return jnp.concatenate([jnp.where(even, mine, got), jnp.where(even, got, mine)], axis=axis)


def tower_gathered(fresh, inputs, tower_in, tower_out, devices, cap):
    same_core = [list(range(0, devices, 2)), list(range(1, devices, 2))]
    rows = tower_out.shape[0]
    cols = tower_out.reshape(rows, devices // 2, 2, -1)
    cols = [cols[:, :, k].reshape(rows, -1) for k in range(2)]
    even = lax.axis_index("worker") % 2 == 0
    half = by_core(jnp.where(even, cols[0], cols[1]), jnp.where(even, cols[1], cols[0]), devices, 0)
    win, wout = [lax.all_gather(w, AXES, axis_index_groups=same_core, tiled=True) for w in (tower_in, half)]
    ins = [(0, win, win.shape[0], None, 0)]
    return step(fresh, inputs, None, ins, [(wout, [])], [0], (0, 0), 1, cap, True)


def per_device(
    states,
    row_of_user,
    event_users,
    event_features,
    feature_table,
    gate_in,
    gate_state,
    tower_in,
    tower_out,
):
    shards = lax.axis_size(AXES)
    events = event_users.shape[0]
    cap = 2 * (events // shards)
    owners, depth = lax.axis_size("owner"), lax.axis_size("worker") // 2
    by_steps = (owners, depth) == (4, 4)
    chips = (owners, depth) if by_steps else None
    requests, slots, *cut = route(
        row_of_user, event_users, event_features, tower_out, shards, cap, states.shape[0], chips
    )
    sent = send_tower(tower_in, *cut, shards) if by_steps else None
    due = sent[2] if by_steps else [()] * 4
    asked = exchange(requests)
    prior = fetch(asked, states, cap, 0, after=due[0])
    inputs = fetch(asked, feature_table, cap, 1, after=(*due[1], prior))
    fresh = cell(prior, inputs, gate_in, gate_state, after=due[2])
    new_states = update(asked, fresh, states, cap, after=due[3])
    both = [[x, send(x, shards, lambda d: d ^ 1)] for x in (fresh, inputs)]
    if by_steps:
        parts = tower_by_steps(*both, sent, tower_in.shape[0], 2 * tower_out.shape[0], cap, new_states)
    else:
        parts = tower_gathered(*both, tower_in, tower_out, shards, cap)
    back = exchange(parts)
    scores = pick(back, slots, cap).reshape(events)
    return (new_states, scores)


def send_tower(tower_in, mine, theirs, devices):
    def ahead(x):
        return send(x, devices, lambda d: (d & ~6) | ((d + 2) & 6))

    def along_x(x):
        return send(x, devices, lambda d: d ^ 8)

    def along_y(x):
        return send(x, devices, lambda d: d ^ 16)

    def plane(x):
        ax, ay = along_x(x), along_y(x)
        half = x.shape[0] // 2
        return x, ax, ay, along_x(ay[:half]), along_y(ax[half:])

    line = [tower_in]
    for _ in range(3):
        line.append(ahead(line[-1]))
    ins = [plane(x) for x in line]
    parts = (2, mine.shape[0] // 2, mine.shape[1])
    rows = [by_core(mine.reshape(parts), theirs.reshape(parts), devices, 1).reshape(-1, mine.shape[1])]
    for _ in range(3):
        rows.append(ahead(rows[-1]))
    outs = plane(jnp.concatenate(rows, axis=0))
    due = [
        (*ins[0][1:3], line[1], rows[1]),
        (*ins[0][3:], *ins[1][1:3], line[2], rows[2]),
        (*ins[1][3:], line[3], rows[3]),
        outs[1:3],
    ]
    return ins, outs, due


def tower_by_steps(fresh, inputs, sent, rows_in, rows_out, cap, done):
    depth = 4
    planes, outs, _ = sent
    half = rows_in // 2

    def ins_of(back, group):
        line, ax, ay, top, bottom = planes[back]
        whole = [(group, a, rows_in, flip, 0) for flip, a in enumerate((line, ax, ay))]
        return whole + [(group, top, half, 3, 0), (group, bottom, half, 3, half)]

    block = 2 * rows_out
    out_parts = [(a, [(back * block, flip, back) for back in range(depth)]) for flip, a in enumerate(outs[:3])]
    out_parts += [(a, [(k * block, 3, 2 * i + k) for k in range(2)]) for i, a in enumerate(outs[3:])]
    score = None
    for backs in ([0, 1], [2], [3]):
        ins = [part for group, back in enumerate(backs) for part in ins_of(back, group)]
        after = (done,) if score is None else ()
        last = backs[-1] == depth - 1
        score = step(fresh, inputs, score, ins, out_parts, backs, (rows_in, rows_out), depth, cap, last, after)
    return score


def solution(mesh):
    placed = (
        P(AXES, None),
        P(),
        P(AXES),
        P(AXES),
        P(),
        P(),
        P(),
        P(AXES, None),
        P(AXES, None),
    )
    return jax.shard_map(
        per_device,
        mesh=mesh,
        in_specs=placed,
        out_specs=(P(AXES, None), P(AXES)),
        check_vma=False,
    )
```

```python
import functools

import jax
import jax.numpy as jnp
from jax import lax
from jax.experimental import pallas as pl
from jax.experimental.pallas import tpu as pltpu
from jax.sharding import PartitionSpec as P

AXES = ("owner", "worker")
LANES = 128
CHUNK = 256
F32 = jnp.float32
BF16 = jnp.bfloat16
I32 = jnp.int32
VMEM = pl.BlockSpec(memory_space=pltpu.VMEM)
ANY = pl.BlockSpec(memory_space=pl.ANY)
HBM = pl.BlockSpec(memory_space=pltpu.HBM)


def iota(shape, axis):
    return lax.broadcasted_iota(I32, shape, axis)


def onehot(mask):
    return jnp.where(mask, 1.0, 0.0).astype(BF16)


def dot(a, b, ca=1, cb=0):
    return lax.dot_general(a, b, (((ca,), (cb,)), ((), ())), preferred_element_type=F32)


def split3(x):
    a = x.astype(BF16)
    r = x - a.astype(F32)
    b = r.astype(BF16)
    return a, b, (r - b.astype(F32)).astype(BF16)


def route_kernel(*refs, shards, cap, row_count, chips):
    n = 4 if chips else 3
    sources, held, sems = refs[:n], refs[-n - 1 : -1], refs[-1]
    copies = [pltpu.make_async_copy(a, b, sems.at[k]) for k, (a, b) in enumerate(zip(sources, held, strict=True))]
    for copy in copies:
        copy.start()
    table_ref, users_ref, feats_ref = held[:3]
    req_ref, slot_ref = refs[n : n + 2]
    if chips:
        mine_ref, theirs_ref = refs[n + 2 : n + 4]
        wout_ref = held[3]
        copies[3].wait()
        owners, depth = chips
        units = wout_ref.shape[1] // (2 * owners * depth)
        rows = wout_ref.shape[0]
        even = lax.axis_index("worker") % 2 == 0
        for place in range(depth):
            for owner in range(owners):
                at = 2 * units * (owner * depth + place)
                a, b = wout_ref[:, at : at + units], wout_ref[:, at + units : at + 2 * units]
                to = units * ((place % (depth // 2)) * owners + owner)
                line = slice((place // (depth // 2)) * rows, (place // (depth // 2) + 1) * rows)
                mine_ref[line, to : to + units] = jnp.where(even, a, b)
                theirs_ref[line, to : to + units] = jnp.where(even, b, a)
    copies[1].wait()
    users = users_ref[...]
    events = users.shape[1]
    high, low = users >> 7, users & 127
    pick = onehot(iota((table_ref.shape[0], events), 0) == high)
    copies[0].wait()
    table = table_ref[...]
    parts = [((table >> (8 * k)) & 255).astype(F32).astype(BF16) for k in range(3)]
    got = dot(jnp.concatenate(parts, axis=1), pick, 0, 0)
    here = iota((LANES, events), 0) == low
    row = jnp.zeros((1, events), F32)
    for k in range(3):
        part = jnp.where(here, got[k * LANES : (k + 1) * LANES], 0.0)
        row = row + float(256**k) * jnp.sum(part, axis=0, keepdims=True)
    row = row.astype(I32)
    device = iota((shards, events), 0)
    first = device * row_count
    mine = (row >= first) & (row < first + row_count)
    hit = jnp.where(mine, 1.0, 0.0)
    target = jnp.sum(jnp.where(mine, device, 0), axis=0, keepdims=True)
    local = row - target * row_count + 1
    before = onehot(iota((events, events), 0) < iota((events, events), 1))
    rank = dot(hit.astype(BF16), before)
    rank = jnp.sum(hit * rank, axis=0, keepdims=True).astype(I32)
    place = onehot(iota((cap, events), 0) == rank)
    copies[2].wait()
    feats = feats_ref[...]
    bytes_of = [(v & 255).astype(F32) for v in (local >> 8, local, feats >> 8, feats)]
    filled = dot(jnp.concatenate([hit * v for v in bytes_of], axis=0).astype(BF16), place, 1, 1)
    q = [filled[k * shards : (k + 1) * shards].astype(I32) for k in range(4)]
    req_ref[:, :cap] = q[0] * 256 + q[1]
    req_ref[:, cap:] = q[2] * 256 + q[3]
    slot_ref[:1, :] = target
    slot_ref[1:, :] = rank


def route(row_of_user, event_users, event_features, tower_out, shards, cap, row_count, chips):
    events = event_users.shape[0]
    arrays = [row_of_user.reshape(-1, LANES), event_users.reshape(1, events), event_features.reshape(1, events)]
    arrays += [tower_out] if chips else []
    rows, hidden = tower_out.shape
    cut = [jax.ShapeDtypeStruct((2 * rows, hidden // 4), BF16)] * 2 if chips else []
    return pl.pallas_call(
        functools.partial(route_kernel, shards=shards, cap=cap, row_count=row_count, chips=chips),
        out_shape=[
            jax.ShapeDtypeStruct((shards, 2 * cap), I32),
            jax.ShapeDtypeStruct((2, events), I32),
            *cut,
        ],
        in_specs=[HBM] * len(arrays),
        out_specs=[VMEM] * (2 + len(cut)),
        scratch_shapes=[pltpu.VMEM(a.shape, a.dtype) for a in arrays] + [pltpu.SemaphoreType.DMA((len(arrays),))],
        compiler_params=pltpu.CompilerParams(vmem_limit_bytes=60 * 2**20),
        cost_estimate=pl.CostEstimate(flops=10**9, bytes_accessed=10**6, transcendentals=0),
        name="route",
    )(*arrays)


def slot_column(asked, n, cap):
    shards = asked.shape[0]
    source = onehot(iota((n, shards), 0) // cap == iota((n, shards), 1))
    place = (iota((n, cap), 0) & (cap - 1)) == iota((n, cap), 1)
    wide = [dot(source, b.astype(F32).astype(BF16)) for b in (asked >> 8, asked & 255)]
    return jnp.sum(jnp.where(place, wide[0] * 256.0 + wide[1], 0.0), axis=1, keepdims=True).astype(I32)


def slot_row(asked, n, cap):
    shards = asked.shape[0]
    place = onehot((iota((cap, n), 1) & (cap - 1)) == iota((cap, n), 0))
    source = iota((shards, n), 1) // cap == iota((shards, n), 0)
    v = asked[:, :cap]
    wide = [dot(b.astype(F32).astype(BF16), place) for b in (v >> 8, v & 255)]
    return jnp.sum(jnp.where(source, wide[0] * 256.0 + wide[1], 0.0), axis=0, keepdims=True).astype(I32) - 1


def sigmoid(x):
    return 0.5 * jnp.tanh(0.5 * x) + 0.5


def fetch_kernel(asked_ref, table_hbm, *refs, cap, column):
    out_ref, table_ref, *low, sem = refs[-3 - (table_hbm.dtype != BF16) :]
    copy = pltpu.make_async_copy(table_hbm, table_ref, sem)
    copy.start()
    n, rows = out_ref.shape[0], table_hbm.shape[0]
    at_row = slot_column(asked_ref[:, column * cap : (column + 1) * cap], n, cap) - (1 - column)
    copy.wait()
    if low:
        low[0][...] = table_ref[...].astype(BF16)
    known = low[0] if low else table_ref
    for k in range(n // CHUNK):
        at = slice(k * CHUNK, (k + 1) * CHUNK)
        out_ref[at, :] = dot(onehot(iota((CHUNK, rows), 1) == at_row[at]), known[...]).astype(BF16)


def fetch(asked, table, cap, column, after=()):
    n, width = asked.shape[0] * cap, table.shape[1]
    low = [] if table.dtype == BF16 else [pltpu.VMEM(table.shape, BF16)]
    return pl.pallas_call(
        functools.partial(fetch_kernel, cap=cap, column=column),
        out_shape=jax.ShapeDtypeStruct((n, width), BF16),
        in_specs=[VMEM, HBM] + [ANY] * len(after),
        out_specs=VMEM,
        scratch_shapes=[pltpu.VMEM(table.shape, table.dtype), *low, pltpu.SemaphoreType.DMA],
        compiler_params=pltpu.CompilerParams(vmem_limit_bytes=24 * 2**20),
        cost_estimate=pl.CostEstimate(flops=10 * n * width * table.shape[0], bytes_accessed=5 * 10**6, transcendentals=0),
        name="fetch",
    )(asked, table, *after)


def cell_kernel(prior_ref, inputs_ref, gin_hbm, gst_hbm, *refs):
    joined_ref, gin_ref, gst_ref, sems = refs[-4:]
    copies = [pltpu.make_async_copy(gst_hbm, gst_ref, sems.at[0]), pltpu.make_async_copy(gin_hbm, gin_ref, sems.at[1])]
    for copy in copies:
        copy.start()
    for copy in copies:
        copy.wait()
    n, width = prior_ref.shape
    for k in range(n // CHUNK):
        at = slice(k * CHUNK, (k + 1) * CHUNK)
        prior = prior_ref[at, :]
        joined_ref[at, width:] = inputs_ref[at, :]
        gh = dot(prior, gst_ref[...])
        gx = dot(inputs_ref[at, :], gin_ref[...])
        reset = sigmoid(gx[:, :width] + gh[:, :width])
        update = sigmoid(gx[:, width : 2 * width] + gh[:, width : 2 * width])
        cand = jnp.tanh(gx[:, 2 * width :] + reset * gh[:, 2 * width :])
        fresh = (1.0 - update) * cand + update * prior.astype(F32)
        joined_ref[at, :width] = fresh.astype(BF16)


def cell(prior, inputs, gate_in, gate_state, after=()):
    n, width = prior.shape
    return pl.pallas_call(
        cell_kernel,
        out_shape=jax.ShapeDtypeStruct((n, 2 * width), BF16),
        in_specs=[VMEM, VMEM, HBM, HBM] + [ANY] * len(after),
        out_specs=VMEM,
        scratch_shapes=[pltpu.VMEM(gate_in.shape, BF16)] * 2 + [pltpu.SemaphoreType.DMA((2,))],
        compiler_params=pltpu.CompilerParams(vmem_limit_bytes=24 * 2**20),
        cost_estimate=pl.CostEstimate(flops=4 * 10**9, bytes_accessed=6 * 10**6, transcendentals=2 * 10**6),
        name="cell",
    )(prior, inputs, gate_in, gate_state, *after)


def update_kernel(asked_ref, joined_ref, states_ref, *refs, cap):
    out_ref, old_ref, new_ref, in_sems, out_sems = refs[-5:]
    n, rows = joined_ref.shape[0], states_ref.shape[0]
    chunks = rows // CHUNK
    parts = [pl.ds(k * CHUNK, CHUNK) for k in range(chunks)]
    reads = [pltpu.make_async_copy(states_ref.at[p], old_ref.at[p], in_sems.at[k]) for k, p in enumerate(parts)]
    writes = [pltpu.make_async_copy(new_ref.at[p], out_ref.at[p], out_sems.at[k]) for k, p in enumerate(parts)]
    for read in reads:
        read.start()
    local = slot_row(asked_ref[...], n, cap)
    fresh = joined_ref[:, : states_ref.shape[1]]
    within = onehot(iota((CHUNK, n), 0) == (local & (CHUNK - 1)))
    counts = dot(within, onehot(iota((chunks, n), 0) * CHUNK == local - (local & (CHUNK - 1))), 1, 1)
    for k in range(chunks):
        at = slice(k * CHUNK, (k + 1) * CHUNK)
        pick = onehot(iota((CHUNK, n), 0) + k * CHUNK == local)
        total = dot(pick, fresh)
        count = counts[:, k : k + 1]
        reads[k].wait()
        old = old_ref[at, :]
        change = total / jnp.maximum(count, 1.0) - old.astype(BF16).astype(F32)
        new_ref[at, :] = old + jnp.where(count > 0.0, change, 0.0)
        writes[k].start()
    for write in writes:
        write.wait()


def update(asked, joined, states, cap, after=()):
    chunks = states.shape[0] // CHUNK
    return pl.pallas_call(
        functools.partial(update_kernel, cap=cap),
        out_shape=jax.ShapeDtypeStruct(states.shape, F32),
        in_specs=[VMEM, VMEM, HBM] + [ANY] * len(after),
        out_specs=HBM,
        scratch_shapes=[pltpu.VMEM(states.shape, F32)] * 2 + [pltpu.SemaphoreType.DMA((chunks,))] * 2,
        compiler_params=pltpu.CompilerParams(vmem_limit_bytes=57 * 2**20),
        cost_estimate=pl.CostEstimate(flops=4 * 10**9, bytes_accessed=10**7, transcendentals=0),
        name="update",
    )(asked, joined, states, *after)


def gelu(x):
    inner = 0.7978845608028654 * (x + 0.044715 * (x * x * x))
    return x * (0.5 * (1.0 + jnp.tanh(inner)))


def owner_at(flip):
    return lax.axis_index("owner") ^ flip


def depth_at(back, depth):
    return lax.rem(lax.axis_index("worker") // 2 + depth - back, depth)


def step_kernel(*refs, n_in, n_out, n_after, ins, outs, backs, rows, depth, cap, first, last):
    it = iter(refs)
    take = lambda k: [next(it) for _ in range(k)]
    sides = take(2)
    before = None if first else next(it)
    in_refs, out_refs = take(n_in), take(n_out)
    take(n_after)
    line_ref, win_ref, wout_ref = take(3)
    groups, width, both = win_ref.shape
    half = both // 2
    chunk = sides[0].shape[0]

    @pl.when(pl.program_id(0) == 0)
    def _():
        for group, index, count, flip, place in ins:
            owner = 0 if flip is None else owner_at(flip)
            at = pl.multiple_of(owner * rows[0] + place, 16)
            win_ref[group, pl.ds(at, count), :] = in_refs[index][...]
        if depth == 1:
            wout_ref[0] = out_refs[0][...]
        else:
            for index, start, flip, back in outs:
                chip = owner_at(flip) * depth + depth_at(back, depth)
                to = pl.ds(pl.multiple_of(chip * rows[1], 16), rows[1])
                for g, group_back in enumerate(backs):
                    place = depth_at(group_back, depth)
                    lanes = pl.ds(pl.multiple_of(lax.rem(place, 2) * width, LANES), width)
                    line = pl.ds(pl.multiple_of(start + rows[1] * (place // 2), 16), rows[1])
                    wout_ref[g, to, :] = out_refs[index][line, lanes]

    near = chunk // cap
    at = pl.ds(pl.multiple_of(pl.program_id(0) * near, near), near)
    for side in range(2):
        joined = sides[side][...]
        tower = jnp.zeros((chunk, half), F32)
        for g in range(groups):
            h = gelu(dot(joined, win_ref[g], 1, 1)).astype(BF16)
            tower = tower + dot(h, wout_ref[g], 1, 1)
        score = jnp.sum(tower * joined[:, half:].astype(F32), axis=1, keepdims=True)
        place = (iota((chunk, cap), 0) & (cap - 1)) == iota((chunk, cap), 1)
        source = onehot(iota((near, chunk), 1) // cap == iota((near, chunk), 0))
        lines = sum(dot(source, p) for p in split3(jnp.where(place, score, 0.0)))
        lanes = slice(side * cap, (side + 1) * cap)
        if not first:
            lines = lines + before[at, lanes]
        if last:
            lines = lines / jnp.sqrt(F32(half))
        line_ref[at, lanes] = lines


def step(sides, before, ins, outs, backs, rows, depth, cap, last, after=()):
    n, half = sides[0].shape[0], sides[0].shape[1] // 2
    shards = n // cap
    chunk = min(n, 2 * CHUNK)
    in_parts = [(group, i, count, flip, place) for i, (group, _, count, flip, place) in enumerate(ins)]
    out_parts = [(i, start, flip, back) for i, (_, parts) in enumerate(outs) for start, flip, back in parts]
    width = sum(count for group, _, count, _, _ in ins if group == 0)
    side = pl.BlockSpec((chunk, 2 * half), lambda i: (i, 0))
    line = pl.BlockSpec((shards, 2 * cap), lambda i: (0, 0))
    whole = lambda a: pl.BlockSpec(a.shape, lambda i: (0, 0))
    units = len(backs) * width
    in_arrays, out_arrays = [a for _, a, _, _, _ in ins], [a for a, _ in outs]
    return pl.pallas_call(
        functools.partial(
            step_kernel,
            n_in=len(in_arrays),
            n_out=len(out_arrays),
            n_after=len(after),
            ins=in_parts,
            outs=out_parts,
            backs=backs,
            rows=rows,
            depth=depth,
            cap=cap,
            first=before is None,
            last=last,
        ),
        grid=(n // chunk,),
        out_shape=jax.ShapeDtypeStruct((shards, 2 * cap), F32),
        in_specs=[side] * 2
        + ([] if before is None else [line])
        + [whole(a) for a in in_arrays + out_arrays]
        + [ANY] * len(after),
        out_specs=line,
        scratch_shapes=[pltpu.VMEM((len(backs), width, 2 * half), BF16), pltpu.VMEM((len(backs), half, width), BF16)],
        compiler_params=pltpu.CompilerParams(vmem_limit_bytes=40 * 2**20),
        cost_estimate=pl.CostEstimate(flops=12 * n * units * half, bytes_accessed=10**7, transcendentals=2 * n * units),
        name="tower",
    )(*sides, *([] if before is None else [before]), *in_arrays, *out_arrays, *after)


def pick_kernel(back_ref, slot_ref, out_ref, *, cap):
    back = back_ref[...]
    shards = back.shape[0]
    target, rank = slot_ref[:1, :], slot_ref[1:, :]
    events = target.shape[1]
    place = onehot(iota((cap, events), 0) == rank)
    device = iota((shards, events), 0)
    score = jnp.zeros((shards, events), F32)
    for side in range(2):
        parts = split3(back[:, side * cap : (side + 1) * cap])
        here = device == (target if side == 0 else target + 1 - 2 * (target & 1))
        score = score + jnp.where(here, sum(dot(p, place) for p in parts), 0.0)
    out_ref[...] = jnp.sum(score, axis=0, keepdims=True)


def pick(back, slots, cap):
    return pl.pallas_call(
        functools.partial(pick_kernel, cap=cap),
        out_shape=jax.ShapeDtypeStruct((1, slots.shape[1]), F32),
        in_specs=[VMEM] * 2,
        out_specs=VMEM,
        compiler_params=pltpu.CompilerParams(vmem_limit_bytes=8 * 2**20),
        cost_estimate=pl.CostEstimate(flops=10**8, bytes_accessed=10**5, transcendentals=0),
        name="pick",
    )(back, slots)


def exchange(x):
    return lax.all_to_all(x, AXES, split_axis=0, concat_axis=0, tiled=True)


def send(x, devices, to):
    return lax.ppermute(x, AXES, [(d, to(d)) for d in range(devices)])


def by_core(mine, theirs, devices, axis):
    even = lax.axis_index("worker") % 2 == 0
    got = send(theirs, devices, lambda d: d ^ 1)
    return jnp.concatenate([jnp.where(even, mine, got), jnp.where(even, got, mine)], axis=axis)


def tower_gathered(sides, tower_in, tower_out, devices, cap):
    same_core = [list(range(0, devices, 2)), list(range(1, devices, 2))]
    rows = tower_out.shape[0]
    cols = tower_out.reshape(rows, devices // 2, 2, -1)
    cols = [cols[:, :, k].reshape(rows, -1) for k in range(2)]
    even = lax.axis_index("worker") % 2 == 0
    half = by_core(jnp.where(even, cols[0], cols[1]), jnp.where(even, cols[1], cols[0]), devices, 0)
    win, wout = [lax.all_gather(w, AXES, axis_index_groups=same_core, tiled=True) for w in (tower_in, half)]
    ins = [(0, win, win.shape[0], None, 0)]
    return step(sides, None, ins, [(wout, [])], [0], (0, 0), 1, cap, True)


def per_device(
    states,
    row_of_user,
    event_users,
    event_features,
    feature_table,
    gate_in,
    gate_state,
    tower_in,
    tower_out,
):
    shards = lax.axis_size(AXES)
    events = event_users.shape[0]
    cap = 2 * (events // shards)
    owners, depth = lax.axis_size("owner"), lax.axis_size("worker") // 2
    by_steps = (owners, depth) == (4, 4)
    chips = (owners, depth) if by_steps else None
    requests, slots, *cut = route(
        row_of_user, event_users, event_features, tower_out, shards, cap, states.shape[0], chips
    )
    tables = (states, feature_table, gate_in, gate_state)
    if by_steps:
        asked, joined, parts = by_waves(requests, cut, tables, tower_in, shards, cap)
    else:
        asked = exchange(requests)
        prior, inputs = fetch(asked, states, cap, 0), fetch(asked, feature_table, cap, 1)
        joined = cell(prior, inputs, gate_in, gate_state)
        sides = [joined, send(joined, shards, lambda d: d ^ 1)]
        parts = tower_gathered(sides, tower_in, tower_out, shards, cap)
    back = exchange(parts)
    new_states = update(asked, joined, states, cap)
    scores = pick(back, slots, cap).reshape(events)
    return (new_states, scores)


def place_kernel(*refs, n, parts):
    sources, outs = refs[:n], refs[-len(parts) :]
    for out, pieces in zip(outs, parts, strict=True):
        to = 0
        for index, start, rows in pieces:
            out[to : to + rows, :] = sources[index][start : start + rows, :]
            to += rows


def place(arrays, parts, after=()):
    cols = arrays[0].shape[1]
    return pl.pallas_call(
        functools.partial(place_kernel, n=len(arrays), parts=parts),
        out_shape=[jax.ShapeDtypeStruct((sum(p[2] for p in ps), cols), arrays[0].dtype) for ps in parts],
        in_specs=[VMEM] * len(arrays) + [ANY] * len(after),
        out_specs=[VMEM] * len(parts),
        compiler_params=pltpu.CompilerParams(vmem_limit_bytes=8 * 2**20),
        cost_estimate=pl.CostEstimate(flops=0, bytes_accessed=10**6, transcendentals=0),
        name="place",
    )(*arrays, *after)


def by_waves(requests, parts, tables, tower_in, devices, cap):
    states, feature_table, gate_in, gate_state = tables

    def ahead(x, places=1):
        return send(x, devices, lambda d: (d & ~6) | ((d + 2 * places) & 6))

    def along_x(x):
        return send(x, devices, lambda d: d ^ 8)

    def along_y(x):
        return send(x, devices, lambda d: d ^ 16)

    def corner(ax, ay, after=()):
        half = ax.shape[0] // 2
        top, bottom = place([ay, ax], [[(0, 0, half)], [(1, half, half)]], after)
        return along_x(top), along_y(bottom)

    mine, theirs = [p.reshape(2, p.shape[0] // 2, p.shape[1]) for p in parts]
    rows = by_core(mine, theirs, devices, 1).reshape(-1, mine.shape[2])
    line = [tower_in]
    for _ in range(3):
        line.append(ahead(line[-1]))
    ax, ay = [along_x(x) for x in line[:3]], [along_y(x) for x in line[:3]]
    asked = exchange(requests)
    n_rows = rows.shape[0]
    line_rows = [rows] + [ahead(rows, k) for k in (1, 2, 3)]
    (all_rows,) = place(line_rows, [[(k, 0, n_rows) for k in range(4)]])
    d = [corner(ax[0], ay[0])]
    rx, ry = along_x(all_rows), along_y(all_rows)
    due = [(), (ax[0], ay[0], line[1]), (rx, ry, ax[1], ay[1], line[2], *d[0])]
    prior = fetch(asked, states, cap, 0, after=due[0])
    inputs = fetch(asked, feature_table, cap, 1, after=(*due[1], prior))
    joined = cell(prior, inputs, gate_in, gate_state, after=due[2])
    d.append(corner(ax[1], ay[1], (joined,)))
    outs = (all_rows, rx, ry, *corner(rx, ry))
    sides = [joined, send(joined, devices, lambda d: d ^ 1)]
    score = None
    for k in range(4):
        plane = (line[k], ax[k], ay[k], *d[k])
        score = tower_step(sides, score, [plane], outs, k, tower_in.shape[0], n_rows // 2, cap)
        if k == 0:
            (late,) = place([line[3]], [[(0, 0, line[3].shape[0])]], (score,))
            ax.append(along_x(late))
            ay.append(along_y(late))
        if k < 2:
            d.append(corner(ax[k + 2], ay[k + 2], (score,)))
    return asked, joined, score


def tower_step(sides, score, planes, outs, first, rows_in, rows_out, cap, after=()):
    depth = 4
    half, block = rows_in // 2, 2 * rows_out
    ins = []
    for group, (here, ax, ay, top, bottom) in enumerate(planes):
        ins += [(group, a, rows_in, flip, 0) for flip, a in enumerate((here, ax, ay))]
        ins += [(group, top, half, 3, 0), (group, bottom, half, 3, half)]
    out_parts = [(a, [(back * block, flip, back) for back in range(depth)]) for flip, a in enumerate(outs[:3])]
    out_parts += [(a, [(k * block, 3, 2 * i + k) for k in range(2)]) for i, a in enumerate(outs[3:])]
    backs = list(range(first, first + len(planes)))
    last = backs[-1] == depth - 1
    return step(sides, score, ins, out_parts, backs, (rows_in, rows_out), depth, cap, last, after)


def solution(mesh):
    placed = (
        P(AXES, None),
        P(),
        P(AXES),
        P(AXES),
        P(),
        P(),
        P(),
        P(AXES, None),
        P(AXES, None),
    )
    return jax.shard_map(
        per_device,
        mesh=mesh,
        in_specs=placed,
        out_specs=(P(AXES, None), P(AXES)),
        check_vma=False,
    )
```

```python
import functools

import jax
import jax.numpy as jnp
from jax import lax
from jax.experimental import pallas as pl
from jax.experimental.pallas import tpu as pltpu
from jax.sharding import PartitionSpec as P

AXES = ("owner", "worker")
LANES = 128
CHUNK = 256
F32 = jnp.float32
BF16 = jnp.bfloat16
I32 = jnp.int32
VMEM = pl.BlockSpec(memory_space=pltpu.VMEM)
ANY = pl.BlockSpec(memory_space=pl.ANY)
HBM = pl.BlockSpec(memory_space=pltpu.HBM)


def iota(shape, axis):
    return lax.broadcasted_iota(I32, shape, axis)


def onehot(mask):
    return jnp.where(mask, 1.0, 0.0).astype(BF16)


def dot(a, b, ca=1, cb=0):
    return lax.dot_general(a, b, (((ca,), (cb,)), ((), ())), preferred_element_type=F32)


def split3(x):
    a = x.astype(BF16)
    r = x - a.astype(F32)
    b = r.astype(BF16)
    return a, b, (r - b.astype(F32)).astype(BF16)


def route_kernel(*refs, shards, cap, row_count, chips):
    n = 4 if chips else 3
    sources, held, sems = refs[:n], refs[-n - 1 : -1], refs[-1]
    copies = [pltpu.make_async_copy(a, b, sems.at[k]) for k, (a, b) in enumerate(zip(sources, held, strict=True))]
    for copy in copies:
        copy.start()
    table_ref, users_ref, feats_ref = held[:3]
    req_ref, slot_ref = refs[n : n + 2]
    if chips:
        mine_ref, theirs_ref = refs[n + 2 : n + 4]
        wout_ref = held[3]
        copies[3].wait()
        owners, depth = chips
        units = wout_ref.shape[1] // (2 * owners * depth)
        rows = wout_ref.shape[0]
        even = lax.axis_index("worker") % 2 == 0
        for place in range(depth):
            for owner in range(owners):
                at = 2 * units * (owner * depth + place)
                a, b = wout_ref[:, at : at + units], wout_ref[:, at + units : at + 2 * units]
                to = units * ((place % (depth // 2)) * owners + owner)
                line = slice((place // (depth // 2)) * rows, (place // (depth // 2) + 1) * rows)
                mine_ref[line, to : to + units] = jnp.where(even, a, b)
                theirs_ref[line, to : to + units] = jnp.where(even, b, a)
    copies[1].wait()
    users = users_ref[...]
    events = users.shape[1]
    high, low = users >> 7, users & 127
    pick = onehot(iota((table_ref.shape[0], events), 0) == high)
    copies[0].wait()
    table = table_ref[...]
    parts = [((table >> (8 * k)) & 255).astype(F32).astype(BF16) for k in range(3)]
    got = dot(jnp.concatenate(parts, axis=1), pick, 0, 0)
    here = iota((LANES, events), 0) == low
    row = jnp.zeros((1, events), F32)
    for k in range(3):
        part = jnp.where(here, got[k * LANES : (k + 1) * LANES], 0.0)
        row = row + float(256**k) * jnp.sum(part, axis=0, keepdims=True)
    row = row.astype(I32)
    device = iota((shards, events), 0)
    first = device * row_count
    mine = (row >= first) & (row < first + row_count)
    hit = jnp.where(mine, 1.0, 0.0)
    target = jnp.sum(jnp.where(mine, device, 0), axis=0, keepdims=True)
    local = row - target * row_count + 1
    before = onehot(iota((events, events), 0) < iota((events, events), 1))
    rank = dot(hit.astype(BF16), before)
    rank = jnp.sum(hit * rank, axis=0, keepdims=True).astype(I32)
    place = onehot(iota((cap, events), 0) == rank)
    copies[2].wait()
    feats = feats_ref[...]
    bytes_of = [(v & 255).astype(F32) for v in (local >> 8, local, feats >> 8, feats)]
    filled = dot(jnp.concatenate([hit * v for v in bytes_of], axis=0).astype(BF16), place, 1, 1)
    q = [filled[k * shards : (k + 1) * shards].astype(I32) for k in range(4)]
    req_ref[:, :cap] = q[0] * 256 + q[1]
    req_ref[:, cap:] = q[2] * 256 + q[3]
    slot_ref[:1, :] = target
    slot_ref[1:, :] = rank


def route(row_of_user, event_users, event_features, tower_out, shards, cap, row_count, chips):
    events = event_users.shape[0]
    arrays = [row_of_user.reshape(-1, LANES), event_users.reshape(1, events), event_features.reshape(1, events)]
    arrays += [tower_out] if chips else []
    rows, hidden = tower_out.shape
    cut = [jax.ShapeDtypeStruct((2 * rows, hidden // 4), BF16)] * 2 if chips else []
    return pl.pallas_call(
        functools.partial(route_kernel, shards=shards, cap=cap, row_count=row_count, chips=chips),
        out_shape=[
            jax.ShapeDtypeStruct((shards, 2 * cap), I32),
            jax.ShapeDtypeStruct((2, events), I32),
            *cut,
        ],
        in_specs=[HBM] * len(arrays),
        out_specs=[VMEM] * (2 + len(cut)),
        scratch_shapes=[pltpu.VMEM(a.shape, a.dtype) for a in arrays] + [pltpu.SemaphoreType.DMA((len(arrays),))],
        compiler_params=pltpu.CompilerParams(vmem_limit_bytes=60 * 2**20),
        cost_estimate=pl.CostEstimate(flops=10**9, bytes_accessed=10**6, transcendentals=0),
        name="route",
    )(*arrays)


def slot_column(asked, n, cap):
    shards = asked.shape[0]
    source = onehot(iota((n, shards), 0) // cap == iota((n, shards), 1))
    place = (iota((n, cap), 0) & (cap - 1)) == iota((n, cap), 1)
    wide = [dot(source, b.astype(F32).astype(BF16)) for b in (asked >> 8, asked & 255)]
    return jnp.sum(jnp.where(place, wide[0] * 256.0 + wide[1], 0.0), axis=1, keepdims=True).astype(I32)


def slot_row(asked, n, cap):
    shards = asked.shape[0]
    place = onehot((iota((cap, n), 1) & (cap - 1)) == iota((cap, n), 0))
    source = iota((shards, n), 1) // cap == iota((shards, n), 0)
    v = asked[:, :cap]
    wide = [dot(b.astype(F32).astype(BF16), place) for b in (v >> 8, v & 255)]
    return jnp.sum(jnp.where(source, wide[0] * 256.0 + wide[1], 0.0), axis=0, keepdims=True).astype(I32) - 1


def sigmoid(x):
    return 0.5 * jnp.tanh(0.5 * x) + 0.5


def fetch_kernel(asked_ref, table_hbm, *refs, cap, column):
    out_ref, table_ref, *low, sem = refs[-3 - (table_hbm.dtype != BF16) :]
    copy = pltpu.make_async_copy(table_hbm, table_ref, sem)
    copy.start()
    n, rows = out_ref.shape[0], table_hbm.shape[0]
    at_row = slot_column(asked_ref[:, column * cap : (column + 1) * cap], n, cap) - (1 - column)
    copy.wait()
    if low:
        low[0][...] = table_ref[...].astype(BF16)
    known = low[0] if low else table_ref
    for k in range(n // CHUNK):
        at = slice(k * CHUNK, (k + 1) * CHUNK)
        out_ref[at, :] = dot(onehot(iota((CHUNK, rows), 1) == at_row[at]), known[...]).astype(BF16)


def fetch(asked, table, cap, column, after=()):
    n, width = asked.shape[0] * cap, table.shape[1]
    low = [] if table.dtype == BF16 else [pltpu.VMEM(table.shape, BF16)]
    return pl.pallas_call(
        functools.partial(fetch_kernel, cap=cap, column=column),
        out_shape=jax.ShapeDtypeStruct((n, width), BF16),
        in_specs=[VMEM, HBM] + [ANY] * len(after),
        out_specs=VMEM,
        scratch_shapes=[pltpu.VMEM(table.shape, table.dtype), *low, pltpu.SemaphoreType.DMA],
        compiler_params=pltpu.CompilerParams(vmem_limit_bytes=24 * 2**20),
        cost_estimate=pl.CostEstimate(flops=10 * n * width * table.shape[0], bytes_accessed=5 * 10**6, transcendentals=0),
        name="fetch",
    )(asked, table, *after)


def cell_kernel(prior_ref, inputs_ref, gin_hbm, gst_hbm, *refs):
    joined_ref, gin_ref, gst_ref, sems = refs[-4:]
    copies = [pltpu.make_async_copy(gst_hbm, gst_ref, sems.at[0]), pltpu.make_async_copy(gin_hbm, gin_ref, sems.at[1])]
    for copy in copies:
        copy.start()
    for copy in copies:
        copy.wait()
    n, width = prior_ref.shape
    for k in range(n // CHUNK):
        at = slice(k * CHUNK, (k + 1) * CHUNK)
        prior = prior_ref[at, :]
        joined_ref[at, width:] = inputs_ref[at, :]
        gh = dot(prior, gst_ref[...])
        gx = dot(inputs_ref[at, :], gin_ref[...])
        reset = sigmoid(gx[:, :width] + gh[:, :width])
        update = sigmoid(gx[:, width : 2 * width] + gh[:, width : 2 * width])
        cand = jnp.tanh(gx[:, 2 * width :] + reset * gh[:, 2 * width :])
        fresh = (1.0 - update) * cand + update * prior.astype(F32)
        joined_ref[at, :width] = fresh.astype(BF16)


def cell(prior, inputs, gate_in, gate_state, after=()):
    n, width = prior.shape
    return pl.pallas_call(
        cell_kernel,
        out_shape=jax.ShapeDtypeStruct((n, 2 * width), BF16),
        in_specs=[VMEM, VMEM, HBM, HBM] + [ANY] * len(after),
        out_specs=VMEM,
        scratch_shapes=[pltpu.VMEM(gate_in.shape, BF16)] * 2 + [pltpu.SemaphoreType.DMA((2,))],
        compiler_params=pltpu.CompilerParams(vmem_limit_bytes=24 * 2**20),
        cost_estimate=pl.CostEstimate(flops=4 * 10**9, bytes_accessed=6 * 10**6, transcendentals=2 * 10**6),
        name="cell",
    )(prior, inputs, gate_in, gate_state, *after)


def update_kernel(asked_ref, joined_ref, states_ref, *refs, cap):
    out_ref, old_ref, new_ref, in_sems, out_sems = refs[-5:]
    n, rows = joined_ref.shape[0], states_ref.shape[0]
    chunks = rows // CHUNK
    parts = [pl.ds(k * CHUNK, CHUNK) for k in range(chunks)]
    reads = [pltpu.make_async_copy(states_ref.at[p], old_ref.at[p], in_sems.at[k]) for k, p in enumerate(parts)]
    writes = [pltpu.make_async_copy(new_ref.at[p], out_ref.at[p], out_sems.at[k]) for k, p in enumerate(parts)]
    for read in reads:
        read.start()
    local = slot_row(asked_ref[...], n, cap)
    fresh = joined_ref[:, : states_ref.shape[1]]
    within = onehot(iota((CHUNK, n), 0) == (local & (CHUNK - 1)))
    counts = dot(within, onehot(iota((chunks, n), 0) * CHUNK == local - (local & (CHUNK - 1))), 1, 1)
    for k in range(chunks):
        at = slice(k * CHUNK, (k + 1) * CHUNK)
        pick = onehot(iota((CHUNK, n), 0) + k * CHUNK == local)
        total = dot(pick, fresh)
        count = counts[:, k : k + 1]
        reads[k].wait()
        old = old_ref[at, :]
        change = total / jnp.maximum(count, 1.0) - old.astype(BF16).astype(F32)
        new_ref[at, :] = old + jnp.where(count > 0.0, change, 0.0)
        writes[k].start()
    for write in writes:
        write.wait()


def update(asked, joined, states, cap, after=()):
    chunks = states.shape[0] // CHUNK
    return pl.pallas_call(
        functools.partial(update_kernel, cap=cap),
        out_shape=jax.ShapeDtypeStruct(states.shape, F32),
        in_specs=[VMEM, VMEM, HBM] + [ANY] * len(after),
        out_specs=HBM,
        scratch_shapes=[pltpu.VMEM(states.shape, F32)] * 2 + [pltpu.SemaphoreType.DMA((chunks,))] * 2,
        compiler_params=pltpu.CompilerParams(vmem_limit_bytes=57 * 2**20),
        cost_estimate=pl.CostEstimate(flops=4 * 10**9, bytes_accessed=10**7, transcendentals=0),
        name="update",
    )(asked, joined, states, *after)


def gelu(x):
    inner = 0.7978845608028654 * (x + 0.044715 * (x * x * x))
    return x * (0.5 * (1.0 + jnp.tanh(inner)))


def owner_at(flip):
    return lax.axis_index("owner") ^ flip


def depth_at(back, depth):
    return lax.rem(lax.axis_index("worker") // 2 + depth - back, depth)


def step_kernel(*refs, n_in, n_out, n_after, ins, outs, backs, rows, depth, cap, first, last):
    it = iter(refs)
    take = lambda k: [next(it) for _ in range(k)]
    sides = take(2)
    before = None if first else next(it)
    in_refs, out_refs = take(n_in), take(n_out)
    take(n_after)
    line_ref, win_ref, wout_ref = take(3)
    groups, width, both = win_ref.shape
    half = both // 2
    chunk = min(sides[0].shape[0], 2 * CHUNK)

    for group, index, count, flip, place in ins:
        owner = 0 if flip is None else owner_at(flip)
        at = pl.multiple_of(owner * rows[0] + place, 16)
        win_ref[group, pl.ds(at, count), :] = in_refs[index][...]
    if depth == 1:
        wout_ref[0] = out_refs[0][...]
    else:
        for index, start, flip, back in outs:
            chip = owner_at(flip) * depth + depth_at(back, depth)
            to = pl.ds(pl.multiple_of(chip * rows[1], 16), rows[1])
            for g, group_back in enumerate(backs):
                place = depth_at(group_back, depth)
                lanes = pl.ds(pl.multiple_of(lax.rem(place, 2) * width, LANES), width)
                line = pl.ds(pl.multiple_of(start + rows[1] * (place // 2), 16), rows[1])
                wout_ref[g, to, :] = out_refs[index][line, lanes]

    near = chunk // cap
    for k in range(sides[0].shape[0] // chunk):
        at = slice(k * near, (k + 1) * near)
        for side in range(2):
            joined = sides[side][k * chunk : (k + 1) * chunk, :]
            tower = jnp.zeros((chunk, half), F32)
            for g in range(groups):
                h = gelu(dot(joined, win_ref[g], 1, 1)).astype(BF16)
                tower = tower + dot(h, wout_ref[g], 1, 1)
            score = jnp.sum(tower * joined[:, half:].astype(F32), axis=1, keepdims=True)
            place = (iota((chunk, cap), 0) & (cap - 1)) == iota((chunk, cap), 1)
            source = onehot(iota((near, chunk), 1) // cap == iota((near, chunk), 0))
            lines = sum(dot(source, p) for p in split3(jnp.where(place, score, 0.0)))
            lanes = slice(side * cap, (side + 1) * cap)
            if not first:
                lines = lines + before[at, lanes]
            if last:
                lines = lines / jnp.sqrt(F32(half))
            line_ref[at, lanes] = lines


def step(sides, before, ins, outs, backs, rows, depth, cap, last, after=()):
    n, half = sides[0].shape[0], sides[0].shape[1] // 2
    shards = n // cap
    in_parts = [(group, i, count, flip, place) for i, (group, _, count, flip, place) in enumerate(ins)]
    out_parts = [(i, start, flip, back) for i, (_, parts) in enumerate(outs) for start, flip, back in parts]
    width = sum(count for group, _, count, _, _ in ins if group == 0)
    units = len(backs) * width
    in_arrays, out_arrays = [a for _, a, _, _, _ in ins], [a for a, _ in outs]
    return pl.pallas_call(
        functools.partial(
            step_kernel,
            n_in=len(in_arrays),
            n_out=len(out_arrays),
            n_after=len(after),
            ins=in_parts,
            outs=out_parts,
            backs=backs,
            rows=rows,
            depth=depth,
            cap=cap,
            first=before is None,
            last=last,
        ),
        out_shape=jax.ShapeDtypeStruct((shards, 2 * cap), F32),
        in_specs=[VMEM] * (2 + (before is not None) + len(in_arrays) + len(out_arrays)) + [ANY] * len(after),
        out_specs=VMEM,
        scratch_shapes=[pltpu.VMEM((len(backs), width, 2 * half), BF16), pltpu.VMEM((len(backs), half, width), BF16)],
        compiler_params=pltpu.CompilerParams(vmem_limit_bytes=40 * 2**20),
        cost_estimate=pl.CostEstimate(flops=12 * n * units * half, bytes_accessed=10**7, transcendentals=2 * n * units),
        name="tower",
    )(*sides, *([] if before is None else [before]), *in_arrays, *out_arrays, *after)


def pick_kernel(back_ref, slot_ref, out_ref, *, cap):
    back = back_ref[...]
    shards = back.shape[0]
    target, rank = slot_ref[:1, :], slot_ref[1:, :]
    events = target.shape[1]
    place = onehot(iota((cap, events), 0) == rank)
    device = iota((shards, events), 0)
    score = jnp.zeros((shards, events), F32)
    for side in range(2):
        parts = split3(back[:, side * cap : (side + 1) * cap])
        here = device == (target if side == 0 else target + 1 - 2 * (target & 1))
        score = score + jnp.where(here, sum(dot(p, place) for p in parts), 0.0)
    out_ref[...] = jnp.sum(score, axis=0, keepdims=True)


def pick(back, slots, cap):
    return pl.pallas_call(
        functools.partial(pick_kernel, cap=cap),
        out_shape=jax.ShapeDtypeStruct((1, slots.shape[1]), F32),
        in_specs=[VMEM] * 2,
        out_specs=VMEM,
        compiler_params=pltpu.CompilerParams(vmem_limit_bytes=8 * 2**20),
        cost_estimate=pl.CostEstimate(flops=10**8, bytes_accessed=10**5, transcendentals=0),
        name="pick",
    )(back, slots)


def exchange(x):
    return lax.all_to_all(x, AXES, split_axis=0, concat_axis=0, tiled=True)


def send(x, devices, to):
    return lax.ppermute(x, AXES, [(d, to(d)) for d in range(devices)])


def by_core(mine, theirs, devices, axis):
    even = lax.axis_index("worker") % 2 == 0
    got = send(theirs, devices, lambda d: d ^ 1)
    return jnp.concatenate([jnp.where(even, mine, got), jnp.where(even, got, mine)], axis=axis)


def tower_gathered(sides, tower_in, tower_out, devices, cap):
    same_core = [list(range(0, devices, 2)), list(range(1, devices, 2))]
    rows = tower_out.shape[0]
    cols = tower_out.reshape(rows, devices // 2, 2, -1)
    cols = [cols[:, :, k].reshape(rows, -1) for k in range(2)]
    even = lax.axis_index("worker") % 2 == 0
    half = by_core(jnp.where(even, cols[0], cols[1]), jnp.where(even, cols[1], cols[0]), devices, 0)
    win, wout = [lax.all_gather(w, AXES, axis_index_groups=same_core, tiled=True) for w in (tower_in, half)]
    ins = [(0, win, win.shape[0], None, 0)]
    return step(sides, None, ins, [(wout, [])], [0], (0, 0), 1, cap, True)


def per_device(
    states,
    row_of_user,
    event_users,
    event_features,
    feature_table,
    gate_in,
    gate_state,
    tower_in,
    tower_out,
):
    shards = lax.axis_size(AXES)
    events = event_users.shape[0]
    cap = 2 * (events // shards)
    owners, depth = lax.axis_size("owner"), lax.axis_size("worker") // 2
    by_steps = (owners, depth) == (4, 4)
    chips = (owners, depth) if by_steps else None
    requests, slots, *cut = route(
        row_of_user, event_users, event_features, tower_out, shards, cap, states.shape[0], chips
    )
    tables = (states, feature_table, gate_in, gate_state)
    if by_steps:
        asked, joined, parts = by_waves(requests, cut, tables, tower_in, shards, cap)
    else:
        asked = exchange(requests)
        prior, inputs = fetch(asked, states, cap, 0), fetch(asked, feature_table, cap, 1)
        joined = cell(prior, inputs, gate_in, gate_state)
        sides = [joined, send(joined, shards, lambda d: d ^ 1)]
        parts = tower_gathered(sides, tower_in, tower_out, shards, cap)
    back = exchange(parts)
    new_states = update(asked, joined, states, cap)
    scores = pick(back, slots, cap).reshape(events)
    return (new_states, scores)


def place_kernel(*refs, n, parts):
    sources, outs = refs[:n], refs[-len(parts) :]
    for out, pieces in zip(outs, parts, strict=True):
        to = 0
        for index, start, rows in pieces:
            out[to : to + rows, :] = sources[index][start : start + rows, :]
            to += rows


def place(arrays, parts, after=()):
    cols = arrays[0].shape[1]
    return pl.pallas_call(
        functools.partial(place_kernel, n=len(arrays), parts=parts),
        out_shape=[jax.ShapeDtypeStruct((sum(p[2] for p in ps), cols), arrays[0].dtype) for ps in parts],
        in_specs=[VMEM] * len(arrays) + [ANY] * len(after),
        out_specs=[VMEM] * len(parts),
        compiler_params=pltpu.CompilerParams(vmem_limit_bytes=8 * 2**20),
        cost_estimate=pl.CostEstimate(flops=0, bytes_accessed=10**6, transcendentals=0),
        name="place",
    )(*arrays, *after)


def by_waves(requests, parts, tables, tower_in, devices, cap):
    states, feature_table, gate_in, gate_state = tables

    def ahead(x, places=1):
        return send(x, devices, lambda d: (d & ~6) | ((d + 2 * places) & 6))

    def along_x(x):
        return send(x, devices, lambda d: d ^ 8)

    def along_y(x):
        return send(x, devices, lambda d: d ^ 16)

    def corner(ax, ay, after=()):
        half = ax.shape[0] // 2
        top, bottom = place([ay, ax], [[(0, 0, half)], [(1, half, half)]], after)
        return along_x(top), along_y(bottom)

    mine, theirs = [p.reshape(2, p.shape[0] // 2, p.shape[1]) for p in parts]
    rows = by_core(mine, theirs, devices, 1).reshape(-1, mine.shape[2])
    line = [tower_in]
    for _ in range(3):
        line.append(ahead(line[-1]))
    ax, ay = [along_x(x) for x in line[:3]], [along_y(x) for x in line[:3]]
    asked = exchange(requests)
    n_rows = rows.shape[0]
    line_rows = [rows] + [ahead(rows, k) for k in (1, 2, 3)]
    (all_rows,) = place(line_rows, [[(k, 0, n_rows) for k in range(4)]])
    d = [corner(ax[0], ay[0])]
    rx, ry = along_x(all_rows), along_y(all_rows)
    due = [(), (ax[0], ay[0], line[1]), (rx, ry, ax[1], ay[1], line[2], *d[0])]
    prior = fetch(asked, states, cap, 0, after=due[0])
    inputs = fetch(asked, feature_table, cap, 1, after=(*due[1], prior))
    joined = cell(prior, inputs, gate_in, gate_state, after=due[2])
    d.append(corner(ax[1], ay[1], (joined,)))
    outs = (all_rows, rx, ry, *corner(rx, ry))
    sides = [joined, send(joined, devices, lambda d: d ^ 1)]
    score = None
    for k in range(4):
        plane = (line[k], ax[k], ay[k], *d[k])
        score = tower_step(sides, score, [plane], outs, k, tower_in.shape[0], n_rows // 2, cap)
        if k == 0:
            (late,) = place([line[3]], [[(0, 0, line[3].shape[0])]], (score,))
            ax.append(along_x(late))
            ay.append(along_y(late))
        if k < 2:
            d.append(corner(ax[k + 2], ay[k + 2], (score,)))
    return asked, joined, score


def tower_step(sides, score, planes, outs, first, rows_in, rows_out, cap, after=()):
    depth = 4
    half, block = rows_in // 2, 2 * rows_out
    ins = []
    for group, (here, ax, ay, top, bottom) in enumerate(planes):
        ins += [(group, a, rows_in, flip, 0) for flip, a in enumerate((here, ax, ay))]
        ins += [(group, top, half, 3, 0), (group, bottom, half, 3, half)]
    out_parts = [(a, [(back * block, flip, back) for back in range(depth)]) for flip, a in enumerate(outs[:3])]
    out_parts += [(a, [(k * block, 3, 2 * i + k) for k in range(2)]) for i, a in enumerate(outs[3:])]
    backs = list(range(first, first + len(planes)))
    last = backs[-1] == depth - 1
    return step(sides, score, ins, out_parts, backs, (rows_in, rows_out), depth, cap, last, after)


def solution(mesh):
    placed = (
        P(AXES, None),
        P(),
        P(AXES),
        P(AXES),
        P(),
        P(),
        P(),
        P(AXES, None),
        P(AXES, None),
    )
    return jax.shard_map(
        per_device,
        mesh=mesh,
        in_specs=placed,
        out_specs=(P(AXES, None), P(AXES)),
        check_vma=False,
    )
```

```python
import functools

import jax
import jax.numpy as jnp
from jax import lax
from jax.experimental import pallas as pl
from jax.experimental.pallas import tpu as pltpu
from jax.sharding import PartitionSpec as P

AXES = ("owner", "worker")
LANES = 128
CHUNK = 256
WIDE = 512
F32 = jnp.float32
BF16 = jnp.bfloat16
I32 = jnp.int32
VMEM = pl.BlockSpec(memory_space=pltpu.VMEM)
ANY = pl.BlockSpec(memory_space=pl.ANY)
HBM = pl.BlockSpec(memory_space=pltpu.HBM)


def iota(shape, axis):
    return lax.broadcasted_iota(I32, shape, axis)


def onehot(mask):
    return jnp.where(mask, 1.0, 0.0).astype(BF16)


def dot(a, b, ca=1, cb=0):
    return lax.dot_general(a, b, (((ca,), (cb,)), ((), ())), preferred_element_type=F32)


def split3(x):
    a = x.astype(BF16)
    r = x - a.astype(F32)
    b = r.astype(BF16)
    return a, b, (r - b.astype(F32)).astype(BF16)


def route_kernel(*refs, shards, cap, row_count, chips):
    n = 4 if chips else 3
    sources, held, sems = refs[:n], refs[-n - 1 : -1], refs[-1]
    copies = [pltpu.make_async_copy(a, b, sems.at[k]) for k, (a, b) in enumerate(zip(sources, held, strict=True))]
    for copy in copies:
        copy.start()
    table_ref, users_ref, feats_ref = held[:3]
    req_ref, slot_ref = refs[n : n + 2]
    if chips:
        mine_ref, theirs_ref = refs[n + 2 : n + 4]
        wout_ref = held[3]
        copies[3].wait()
        owners, depth = chips
        units = wout_ref.shape[1] // (2 * owners * depth)
        rows = wout_ref.shape[0]
        even = lax.axis_index("worker") % 2 == 0
        for place in range(depth):
            for owner in range(owners):
                at = 2 * units * (owner * depth + place)
                a, b = wout_ref[:, at : at + units], wout_ref[:, at + units : at + 2 * units]
                to = units * ((place % (depth // 2)) * owners + owner)
                line = slice((place // (depth // 2)) * rows, (place // (depth // 2) + 1) * rows)
                mine_ref[line, to : to + units] = jnp.where(even, a, b)
                theirs_ref[line, to : to + units] = jnp.where(even, b, a)
    copies[1].wait()
    users = users_ref[...]
    events = users.shape[1]
    high, low = users >> 7, users & 127
    pick = onehot(iota((table_ref.shape[0], events), 0) == high)
    copies[0].wait()
    table = table_ref[...]
    parts = [((table >> (8 * k)) & 255).astype(F32).astype(BF16) for k in range(3)]
    got = dot(jnp.concatenate(parts, axis=1), pick, 0, 0)
    here = iota((LANES, events), 0) == low
    row = jnp.zeros((1, events), F32)
    for k in range(3):
        part = jnp.where(here, got[k * LANES : (k + 1) * LANES], 0.0)
        row = row + float(256**k) * jnp.sum(part, axis=0, keepdims=True)
    row = row.astype(I32)
    device = iota((shards, events), 0)
    first = device * row_count
    mine = (row >= first) & (row < first + row_count)
    hit = jnp.where(mine, 1.0, 0.0)
    target = jnp.sum(jnp.where(mine, device, 0), axis=0, keepdims=True)
    local = row - target * row_count + 1
    before = onehot(iota((events, events), 0) < iota((events, events), 1))
    rank = dot(hit.astype(BF16), before)
    rank = jnp.sum(hit * rank, axis=0, keepdims=True).astype(I32)
    place = onehot(iota((cap, events), 0) == rank)
    copies[2].wait()
    feats = feats_ref[...]
    bytes_of = [(v & 255).astype(F32) for v in (local >> 8, local, feats >> 8, feats)]
    filled = dot(jnp.concatenate([hit * v for v in bytes_of], axis=0).astype(BF16), place, 1, 1)
    q = [filled[k * shards : (k + 1) * shards].astype(I32) for k in range(4)]
    req_ref[:, :cap] = q[0] * 256 + q[1]
    req_ref[:, cap:] = q[2] * 256 + q[3]
    slot_ref[:1, :] = target
    slot_ref[1:, :] = rank


def route(row_of_user, event_users, event_features, tower_out, shards, cap, row_count, chips):
    events = event_users.shape[0]
    arrays = [row_of_user.reshape(-1, LANES), event_users.reshape(1, events), event_features.reshape(1, events)]
    arrays += [tower_out] if chips else []
    rows, hidden = tower_out.shape
    cut = [jax.ShapeDtypeStruct((2 * rows, hidden // 4), BF16)] * 2 if chips else []
    return pl.pallas_call(
        functools.partial(route_kernel, shards=shards, cap=cap, row_count=row_count, chips=chips),
        out_shape=[
            jax.ShapeDtypeStruct((shards, 2 * cap), I32),
            jax.ShapeDtypeStruct((2, events), I32),
            *cut,
        ],
        in_specs=[HBM] * len(arrays),
        out_specs=[VMEM] * (2 + len(cut)),
        scratch_shapes=[pltpu.VMEM(a.shape, a.dtype) for a in arrays] + [pltpu.SemaphoreType.DMA((len(arrays),))],
        compiler_params=pltpu.CompilerParams(vmem_limit_bytes=60 * 2**20),
        cost_estimate=pl.CostEstimate(flops=10**9, bytes_accessed=10**6, transcendentals=0),
        name="route",
    )(*arrays)


def slot_column(asked, n, cap):
    shards = asked.shape[0]
    source = onehot(iota((n, shards), 0) // cap == iota((n, shards), 1))
    place = (iota((n, cap), 0) & (cap - 1)) == iota((n, cap), 1)
    wide = [dot(source, b.astype(F32).astype(BF16)) for b in (asked >> 8, asked & 255)]
    return jnp.sum(jnp.where(place, wide[0] * 256.0 + wide[1], 0.0), axis=1, keepdims=True).astype(I32)


def slot_row(asked, n, cap):
    shards = asked.shape[0]
    place = onehot((iota((cap, n), 1) & (cap - 1)) == iota((cap, n), 0))
    source = iota((shards, n), 1) // cap == iota((shards, n), 0)
    v = asked[:, :cap]
    wide = [dot(b.astype(F32).astype(BF16), place) for b in (v >> 8, v & 255)]
    return jnp.sum(jnp.where(source, wide[0] * 256.0 + wide[1], 0.0), axis=0, keepdims=True).astype(I32) - 1


def sigmoid(x):
    return 0.5 * jnp.tanh(0.5 * x) + 0.5


def fetch_kernel(asked_ref, table_hbm, *refs, cap, column):
    out_ref, table_ref, *low, sem = refs[-3 - (table_hbm.dtype != BF16) :]
    copy = pltpu.make_async_copy(table_hbm, table_ref, sem)
    copy.start()
    n, rows = out_ref.shape[0], table_hbm.shape[0]
    at_row = slot_column(asked_ref[:, column * cap : (column + 1) * cap], n, cap) - (1 - column)
    copy.wait()
    if low:
        low[0][...] = table_ref[...].astype(BF16)
    known = low[0] if low else table_ref
    for k in range(n // CHUNK):
        at = slice(k * CHUNK, (k + 1) * CHUNK)
        out_ref[at, :] = dot(onehot(iota((CHUNK, rows), 1) == at_row[at]), known[...]).astype(BF16)


def fetch(asked, table, cap, column, after=()):
    n, width = asked.shape[0] * cap, table.shape[1]
    low = [] if table.dtype == BF16 else [pltpu.VMEM(table.shape, BF16)]
    return pl.pallas_call(
        functools.partial(fetch_kernel, cap=cap, column=column),
        out_shape=jax.ShapeDtypeStruct((n, width), BF16),
        in_specs=[VMEM, HBM] + [ANY] * len(after),
        out_specs=VMEM,
        scratch_shapes=[pltpu.VMEM(table.shape, table.dtype), *low, pltpu.SemaphoreType.DMA],
        compiler_params=pltpu.CompilerParams(vmem_limit_bytes=24 * 2**20),
        cost_estimate=pl.CostEstimate(flops=10 * n * width * table.shape[0], bytes_accessed=5 * 10**6, transcendentals=0),
        name="fetch",
    )(asked, table, *after)


def cell_kernel(prior_ref, inputs_ref, gin_hbm, gst_hbm, *refs):
    joined_ref, gin_ref, gst_ref, sems = refs[-4:]
    copies = [pltpu.make_async_copy(gst_hbm, gst_ref, sems.at[0]), pltpu.make_async_copy(gin_hbm, gin_ref, sems.at[1])]
    for copy in copies:
        copy.start()
    for copy in copies:
        copy.wait()
    n, width = prior_ref.shape
    for k in range(n // WIDE):
        at = slice(k * WIDE, (k + 1) * WIDE)
        prior = prior_ref[at, :]
        joined_ref[at, width:] = inputs_ref[at, :]
        gh = dot(prior, gst_ref[...])
        gx = dot(inputs_ref[at, :], gin_ref[...])
        reset = sigmoid(gx[:, :width] + gh[:, :width])
        update = sigmoid(gx[:, width : 2 * width] + gh[:, width : 2 * width])
        cand = jnp.tanh(gx[:, 2 * width :] + reset * gh[:, 2 * width :])
        fresh = (1.0 - update) * cand + update * prior.astype(F32)
        joined_ref[at, :width] = fresh.astype(BF16)


def cell(prior, inputs, gate_in, gate_state, after=()):
    n, width = prior.shape
    return pl.pallas_call(
        cell_kernel,
        out_shape=jax.ShapeDtypeStruct((n, 2 * width), BF16),
        in_specs=[VMEM, VMEM, HBM, HBM] + [ANY] * len(after),
        out_specs=VMEM,
        scratch_shapes=[pltpu.VMEM(gate_in.shape, BF16)] * 2 + [pltpu.SemaphoreType.DMA((2,))],
        compiler_params=pltpu.CompilerParams(vmem_limit_bytes=24 * 2**20),
        cost_estimate=pl.CostEstimate(flops=4 * 10**9, bytes_accessed=6 * 10**6, transcendentals=2 * 10**6),
        name="cell",
    )(prior, inputs, gate_in, gate_state, *after)


def update_kernel(asked_ref, joined_ref, states_ref, *refs, cap):
    out_ref, old_ref, new_ref, in_sems, out_sems = refs[-5:]
    n, rows = joined_ref.shape[0], states_ref.shape[0]
    chunks = rows // CHUNK
    parts = [pl.ds(k * CHUNK, CHUNK) for k in range(chunks)]
    reads = [pltpu.make_async_copy(states_ref.at[p], old_ref.at[p], in_sems.at[k]) for k, p in enumerate(parts)]
    writes = [pltpu.make_async_copy(new_ref.at[p], out_ref.at[p], out_sems.at[k]) for k, p in enumerate(parts)]
    for read in reads:
        read.start()
    local = slot_row(asked_ref[...], n, cap)
    fresh = joined_ref[:, : states_ref.shape[1]]
    within = onehot(iota((CHUNK, n), 0) == (local & (CHUNK - 1)))
    counts = dot(within, onehot(iota((chunks, n), 0) * CHUNK == local - (local & (CHUNK - 1))), 1, 1)
    for k in range(chunks):
        at = slice(k * CHUNK, (k + 1) * CHUNK)
        pick = onehot(iota((CHUNK, n), 0) + k * CHUNK == local)
        total = dot(pick, fresh)
        count = counts[:, k : k + 1]
        reads[k].wait()
        old = old_ref[at, :]
        change = total / jnp.maximum(count, 1.0) - old.astype(BF16).astype(F32)
        new_ref[at, :] = old + jnp.where(count > 0.0, change, 0.0)
        writes[k].start()
    for write in writes:
        write.wait()


def update(asked, joined, states, cap, after=()):
    chunks = states.shape[0] // CHUNK
    return pl.pallas_call(
        functools.partial(update_kernel, cap=cap),
        out_shape=jax.ShapeDtypeStruct(states.shape, F32),
        in_specs=[VMEM, VMEM, HBM] + [ANY] * len(after),
        out_specs=HBM,
        scratch_shapes=[pltpu.VMEM(states.shape, F32)] * 2 + [pltpu.SemaphoreType.DMA((chunks,))] * 2,
        compiler_params=pltpu.CompilerParams(vmem_limit_bytes=57 * 2**20),
        cost_estimate=pl.CostEstimate(flops=4 * 10**9, bytes_accessed=10**7, transcendentals=0),
        name="update",
    )(asked, joined, states, *after)


def gelu(x):
    inner = 0.7978845608028654 * (x + 0.044715 * (x * x * x))
    return x * (0.5 * (1.0 + jnp.tanh(inner)))


def owner_at(flip):
    return lax.axis_index("owner") ^ flip


def depth_at(back, depth):
    return lax.rem(lax.axis_index("worker") // 2 + depth - back, depth)


def step_kernel(*refs, n_in, n_out, n_after, ins, outs, backs, rows, depth, cap, first, last):
    it = iter(refs)
    take = lambda k: [next(it) for _ in range(k)]
    sides = take(2)
    before = None if first else next(it)
    in_refs, out_refs = take(n_in), take(n_out)
    take(n_after)
    line_ref, win_ref, wout_ref = take(3)
    groups, width, both = win_ref.shape
    half = both // 2
    chunk = min(sides[0].shape[0], 2 * CHUNK)

    for group, index, count, flip, place in ins:
        owner = 0 if flip is None else owner_at(flip)
        at = pl.multiple_of(owner * rows[0] + place, 16)
        win_ref[group, pl.ds(at, count), :] = in_refs[index][...]
    if depth == 1:
        wout_ref[0] = out_refs[0][...]
    else:
        for index, start, flip, back in outs:
            chip = owner_at(flip) * depth + depth_at(back, depth)
            to = pl.ds(pl.multiple_of(chip * rows[1], 16), rows[1])
            for g, group_back in enumerate(backs):
                place = depth_at(group_back, depth)
                lanes = pl.ds(pl.multiple_of(lax.rem(place, 2) * width, LANES), width)
                line = pl.ds(pl.multiple_of(start + rows[1] * (place // 2), 16), rows[1])
                wout_ref[g, to, :] = out_refs[index][line, lanes]

    near = chunk // cap
    for k in range(sides[0].shape[0] // chunk):
        at = slice(k * near, (k + 1) * near)
        for side in range(2):
            joined = sides[side][k * chunk : (k + 1) * chunk, :]
            tower = jnp.zeros((chunk, half), F32)
            for g in range(groups):
                h = gelu(dot(joined, win_ref[g], 1, 1)).astype(BF16)
                tower = tower + dot(h, wout_ref[g], 1, 1)
            score = jnp.sum(tower * joined[:, half:].astype(F32), axis=1, keepdims=True)
            place = (iota((chunk, cap), 0) & (cap - 1)) == iota((chunk, cap), 1)
            source = onehot(iota((near, chunk), 1) // cap == iota((near, chunk), 0))
            lines = sum(dot(source, p) for p in split3(jnp.where(place, score, 0.0)))
            lanes = slice(side * cap, (side + 1) * cap)
            if not first:
                lines = lines + before[at, lanes]
            if last:
                lines = lines / jnp.sqrt(F32(half))
            line_ref[at, lanes] = lines


def step(sides, before, ins, outs, backs, rows, depth, cap, last, after=()):
    n, half = sides[0].shape[0], sides[0].shape[1] // 2
    shards = n // cap
    in_parts = [(group, i, count, flip, place) for i, (group, _, count, flip, place) in enumerate(ins)]
    out_parts = [(i, start, flip, back) for i, (_, parts) in enumerate(outs) for start, flip, back in parts]
    width = sum(count for group, _, count, _, _ in ins if group == 0)
    units = len(backs) * width
    in_arrays, out_arrays = [a for _, a, _, _, _ in ins], [a for a, _ in outs]
    return pl.pallas_call(
        functools.partial(
            step_kernel,
            n_in=len(in_arrays),
            n_out=len(out_arrays),
            n_after=len(after),
            ins=in_parts,
            outs=out_parts,
            backs=backs,
            rows=rows,
            depth=depth,
            cap=cap,
            first=before is None,
            last=last,
        ),
        out_shape=jax.ShapeDtypeStruct((shards, 2 * cap), F32),
        in_specs=[VMEM] * (2 + (before is not None) + len(in_arrays) + len(out_arrays)) + [ANY] * len(after),
        out_specs=VMEM,
        scratch_shapes=[pltpu.VMEM((len(backs), width, 2 * half), BF16), pltpu.VMEM((len(backs), half, width), BF16)],
        compiler_params=pltpu.CompilerParams(vmem_limit_bytes=40 * 2**20),
        cost_estimate=pl.CostEstimate(flops=12 * n * units * half, bytes_accessed=10**7, transcendentals=2 * n * units),
        name="tower",
    )(*sides, *([] if before is None else [before]), *in_arrays, *out_arrays, *after)


def pick_kernel(back_ref, slot_ref, out_ref, *, cap):
    back = back_ref[...]
    shards = back.shape[0]
    target, rank = slot_ref[:1, :], slot_ref[1:, :]
    events = target.shape[1]
    place = onehot(iota((cap, events), 0) == rank)
    device = iota((shards, events), 0)
    score = jnp.zeros((shards, events), F32)
    for side in range(2):
        parts = split3(back[:, side * cap : (side + 1) * cap])
        here = device == (target if side == 0 else target + 1 - 2 * (target & 1))
        score = score + jnp.where(here, sum(dot(p, place) for p in parts), 0.0)
    out_ref[...] = jnp.sum(score, axis=0, keepdims=True)


def pick(back, slots, cap):
    return pl.pallas_call(
        functools.partial(pick_kernel, cap=cap),
        out_shape=jax.ShapeDtypeStruct((1, slots.shape[1]), F32),
        in_specs=[VMEM] * 2,
        out_specs=VMEM,
        compiler_params=pltpu.CompilerParams(vmem_limit_bytes=8 * 2**20),
        cost_estimate=pl.CostEstimate(flops=10**8, bytes_accessed=10**5, transcendentals=0),
        name="pick",
    )(back, slots)


def exchange(x):
    return lax.all_to_all(x, AXES, split_axis=0, concat_axis=0, tiled=True)


def send(x, devices, to):
    return lax.ppermute(x, AXES, [(d, to(d)) for d in range(devices)])


def by_core(mine, theirs, devices, axis):
    even = lax.axis_index("worker") % 2 == 0
    got = send(theirs, devices, lambda d: d ^ 1)
    return jnp.concatenate([jnp.where(even, mine, got), jnp.where(even, got, mine)], axis=axis)


def tower_gathered(sides, tower_in, tower_out, devices, cap):
    same_core = [list(range(0, devices, 2)), list(range(1, devices, 2))]
    rows = tower_out.shape[0]
    cols = tower_out.reshape(rows, devices // 2, 2, -1)
    cols = [cols[:, :, k].reshape(rows, -1) for k in range(2)]
    even = lax.axis_index("worker") % 2 == 0
    half = by_core(jnp.where(even, cols[0], cols[1]), jnp.where(even, cols[1], cols[0]), devices, 0)
    win, wout = [lax.all_gather(w, AXES, axis_index_groups=same_core, tiled=True) for w in (tower_in, half)]
    ins = [(0, win, win.shape[0], None, 0)]
    return step(sides, None, ins, [(wout, [])], [0], (0, 0), 1, cap, True)


def per_device(
    states,
    row_of_user,
    event_users,
    event_features,
    feature_table,
    gate_in,
    gate_state,
    tower_in,
    tower_out,
):
    shards = lax.axis_size(AXES)
    events = event_users.shape[0]
    cap = 2 * (events // shards)
    owners, depth = lax.axis_size("owner"), lax.axis_size("worker") // 2
    by_steps = (owners, depth) == (4, 4)
    chips = (owners, depth) if by_steps else None
    requests, slots, *cut = route(
        row_of_user, event_users, event_features, tower_out, shards, cap, states.shape[0], chips
    )
    tables = (states, feature_table, gate_in, gate_state)
    if by_steps:
        asked, joined, parts = by_waves(requests, cut, tables, tower_in, shards, cap)
    else:
        asked = exchange(requests)
        prior, inputs = fetch(asked, states, cap, 0), fetch(asked, feature_table, cap, 1)
        joined = cell(prior, inputs, gate_in, gate_state)
        sides = [joined, send(joined, shards, lambda d: d ^ 1)]
        parts = tower_gathered(sides, tower_in, tower_out, shards, cap)
    back = exchange(parts)
    new_states = update(asked, joined, states, cap)
    scores = pick(back, slots, cap).reshape(events)
    return (new_states, scores)


def place_kernel(*refs, n, parts):
    sources, outs = refs[:n], refs[-len(parts) :]
    for out, pieces in zip(outs, parts, strict=True):
        to = 0
        for index, start, rows in pieces:
            out[to : to + rows, :] = sources[index][start : start + rows, :]
            to += rows


def place(arrays, parts, after=()):
    cols = arrays[0].shape[1]
    return pl.pallas_call(
        functools.partial(place_kernel, n=len(arrays), parts=parts),
        out_shape=[jax.ShapeDtypeStruct((sum(p[2] for p in ps), cols), arrays[0].dtype) for ps in parts],
        in_specs=[VMEM] * len(arrays) + [ANY] * len(after),
        out_specs=[VMEM] * len(parts),
        compiler_params=pltpu.CompilerParams(vmem_limit_bytes=8 * 2**20),
        cost_estimate=pl.CostEstimate(flops=0, bytes_accessed=10**6, transcendentals=0),
        name="place",
    )(*arrays, *after)


def by_waves(requests, parts, tables, tower_in, devices, cap):
    states, feature_table, gate_in, gate_state = tables

    def ahead(x, places=1):
        return send(x, devices, lambda d: (d & ~6) | ((d + 2 * places) & 6))

    def along_x(x):
        return send(x, devices, lambda d: d ^ 8)

    def along_y(x):
        return send(x, devices, lambda d: d ^ 16)

    def corner(ax, ay, after=()):
        half = ax.shape[0] // 2
        top, bottom = place([ay, ax], [[(0, 0, half)], [(1, half, half)]], after)
        return along_x(top), along_y(bottom)

    mine, theirs = [p.reshape(2, p.shape[0] // 2, p.shape[1]) for p in parts]
    rows = by_core(mine, theirs, devices, 1).reshape(-1, mine.shape[2])
    line = [tower_in]
    for _ in range(3):
        line.append(ahead(line[-1]))
    ax, ay = [along_x(x) for x in line[:3]], [along_y(x) for x in line[:3]]
    asked = exchange(requests)
    n_rows = rows.shape[0]
    line_rows = [rows] + [ahead(rows, k) for k in (1, 2, 3)]
    (all_rows,) = place(line_rows, [[(k, 0, n_rows) for k in range(4)]])
    d = [corner(ax[0], ay[0])]
    rx, ry = along_x(all_rows), along_y(all_rows)
    due = [(), (ax[0], ay[0], line[1]), (rx, ry, ax[1], ay[1], line[2], *d[0])]
    prior = fetch(asked, states, cap, 0, after=due[0])
    inputs = fetch(asked, feature_table, cap, 1, after=(*due[1], prior))
    joined = cell(prior, inputs, gate_in, gate_state, after=due[2])
    d.append(corner(ax[1], ay[1], (joined,)))
    outs = (all_rows, rx, ry, *corner(rx, ry))
    sides = [joined, send(joined, devices, lambda d: d ^ 1)]
    score = None
    for k in range(4):
        plane = (line[k], ax[k], ay[k], *d[k])
        score = tower_step(sides, score, [plane], outs, k, tower_in.shape[0], n_rows // 2, cap)
        if k == 0:
            (late,) = place([line[3]], [[(0, 0, line[3].shape[0])]], (score,))
            ax.append(along_x(late))
            ay.append(along_y(late))
        if k < 2:
            d.append(corner(ax[k + 2], ay[k + 2], (score,)))
    return asked, joined, score


def tower_step(sides, score, planes, outs, first, rows_in, rows_out, cap, after=()):
    depth = 4
    half, block = rows_in // 2, 2 * rows_out
    ins = []
    for group, (here, ax, ay, top, bottom) in enumerate(planes):
        ins += [(group, a, rows_in, flip, 0) for flip, a in enumerate((here, ax, ay))]
        ins += [(group, top, half, 3, 0), (group, bottom, half, 3, half)]
    out_parts = [(a, [(back * block, flip, back) for back in range(depth)]) for flip, a in enumerate(outs[:3])]
    out_parts += [(a, [(k * block, 3, 2 * i + k) for k in range(2)]) for i, a in enumerate(outs[3:])]
    backs = list(range(first, first + len(planes)))
    last = backs[-1] == depth - 1
    return step(sides, score, ins, out_parts, backs, (rows_in, rows_out), depth, cap, last, after)


def solution(mesh):
    placed = (
        P(AXES, None),
        P(),
        P(AXES),
        P(AXES),
        P(),
        P(),
        P(),
        P(AXES, None),
        P(AXES, None),
    )
    return jax.shard_map(
        per_device,
        mesh=mesh,
        in_specs=placed,
        out_specs=(P(AXES, None), P(AXES)),
        check_vma=False,
    )
```
